128 devices in a mesh: grp: 4 (over z), dev: 32 (over y, x, core).
Axes of the slice: x: 4, y: 4, z: 4, core: 2. Of those that a mesh axis runs over, the one named last changes fastest.
Arguments:
- near_blocks: bfloat16 [512, 6, 512, 512], P(('grp', 'dev')), may hold values from -0.109375 to 0.109375
- samples: bfloat16 [262144, 256], P(('grp', 'dev')), may hold values from -6 to 6
- pattern: int32 [512, 5], P(('grp', 'dev')), may hold values from 0 to 511, as said below
Outputs:
- leaf_bases: float32 [262144, 256], P(('grp', 'dev'))
- transfers: float32 [512, 512, 256], P(('grp', 'dev'))
- root_factor: float32 [256, 256], replicated
The draws below stay inside these ranges and needn't reach their ends.
Inputs may be any that keep to these rules, and one draw needn't show every extreme that they name: pattern[i, s] lies within 4 leaves of leaf i.
All inputs are finite; a program needn't handle non-finite values.
Results may differ from the reference program's by a relative error of at most 0.0003.
Values may be sent and summed in bfloat16 or wider, within the bound.
No kernel may reach another device: no remote copies, remote signals or barrier semaphores. Data moves between devices by JAX's collectives and lax.ppermute only.
A program may use at most 192 MiB of HBM per device.

```python
import math
import jax
import jax.numpy as jnp
from jax import lax

LEAF = 512
RANK = 256
NB = 6
NEAR = 4
NLEAF = 512
ROWS = 262144


def draw_pattern(key, part):
    key = jax.random.fold_in(key, 7)
    offset_span = 2 * NEAR
    scores = jax.random.randint(key, (NLEAF, offset_span), 0, 1 << 20) * offset_span
    scores = scores + jnp.arange(offset_span, dtype=jnp.int32)[None, :]
    ranked = jnp.argsort(scores, axis=1)
    chosen = ranked[:, :NB - 1].astype(jnp.int32)
    offsets = jnp.where(chosen < NEAR, chosen - NEAR, chosen - NEAR + 1)
    row_ids = jnp.arange(NLEAF, dtype=jnp.int32)[:, None]
    column_ids = jnp.clip(row_ids + offsets, 0, NLEAF - 1)
    return column_ids.astype(jnp.int32)


def draw_samples(key, part):
    key = jax.random.fold_in(key, 11)
    scale_key, value_key = jax.random.split(key)
    column_scales = jnp.exp(jax.random.uniform(scale_key, (RANK,), jnp.float32, -3.5, 0.0))
    values = jnp.clip(jax.random.normal(value_key, (ROWS, RANK), jnp.float32), -6.0, 6.0)
    return (values * column_scales[None, :]).astype(jnp.bfloat16)


def shard_levels(own_key, extent, cuts, smallest, top_value):
    def one(dim, shards_of):
        draws = jax.random.uniform(jax.random.fold_in(jax.random.fold_in(own_key, 6), dim), (shards_of,), jnp.float32, smallest / len(cuts), top_value / len(cuts))
        return jnp.repeat(jnp.exp(draws), extent[dim] // shards_of).reshape((-1,) + (1,) * (len(extent) - dim - 1))

    gain = one(*cuts[0])
    for cut in cuts[1:]:
        gain = gain * one(*cut)
    return gain


def normal_values(own_key, shape, deviation, most, shards=(), kind=jnp.bfloat16):
    factor_of = shard_levels(own_key, shape, shards, -0.22, 0.18) if shards else 1.0
    drawn = jax.random.normal(own_key, shape, jnp.float32) * deviation * factor_of
    return jnp.minimum(jnp.maximum(drawn, -most), most).astype(kind)


def setup_inputs(seed: int = 0) -> dict:
    key_of = jax.random.split(jax.random.key(seed), 4)
    return {
        "near_blocks": normal_values(key_of[0], (NLEAF, NB, LEAF, LEAF), (NB * LEAF) ** -0.5, 0.109375, ((0, 128),)),
        "samples": draw_samples(jax.random.fold_in(key_of[3], 71), 0),
        "pattern": draw_pattern(jax.random.fold_in(key_of[3], 71), 0),
    }


newton_steps = 10

def product(left, right):
    return jnp.einsum('...rs,...st->...rt', left, right, precision=lax.Precision.HIGHEST)

def orthonormalize(stacked):
    gram_matrix = jnp.einsum('...ir,...is->...rs', stacked, stacked, precision=lax.Precision.HIGHEST)
    norm_scale = jnp.sqrt(lax.optimization_barrier(jnp.sum(gram_matrix * gram_matrix, axis=(-2, -1), keepdims=True))) + 1e-06
    identity = jnp.eye(stacked.shape[-1], dtype=jnp.float32)
    approx = gram_matrix / norm_scale
    inverse = jnp.broadcast_to(identity, approx.shape)
    for step in range(newton_steps):
        middle = 1.5 * identity - 0.5 * product(approx, inverse)
        inverse = product(inverse, middle)
        approx = product(middle, approx)
    root_scale = jnp.sqrt(norm_scale)
    basis = jnp.einsum('...ir,...rs->...is', stacked, inverse, precision=lax.Precision.HIGHEST) / root_scale
    return (basis, approx * root_scale)

def reference(near_blocks, samples, pattern):
    leaves = samples.reshape(NLEAF, LEAF, RANK)
    own_ids = jnp.arange(NLEAF, dtype=jnp.int32)[:, None]
    columns = jnp.concatenate([own_ids, pattern.astype(jnp.int32)], axis=1)

    def leaf_sample(leaf_args):
        blocks, column_ids = leaf_args
        picked = leaves[column_ids]
        return jnp.einsum('sij,sjr->ir', blocks.astype(jnp.float32), picked.astype(jnp.float32))
    sampled = lax.map(leaf_sample, (near_blocks, columns))
    leaf_bases, current = orthonormalize(sampled)
    transfers = jnp.zeros((NLEAF, 2 * RANK, RANK), jnp.float32)
    span_now = 1
    for height in range(NLEAF.bit_length() - 1):
        stacked = current.reshape(current.shape[0] // 2, 2 * RANK, RANK)
        merged, current = orthonormalize(stacked)
        span_now = span_now * 2
        splits = jnp.arange(stacked.shape[0], dtype=jnp.int32) * span_now + span_now // 2
        transfers = transfers.at[splits].set(merged)
    root_factor = current[0] / math.sqrt(ROWS)
    return (leaf_bases.reshape(NLEAF * LEAF, RANK), transfers, root_factor)
```

```python
import math

import jax
import jax.numpy as jnp
from jax import lax
from jax.experimental import pallas as pl
from jax.experimental.pallas import tpu as pltpu
from jax.sharding import PartitionSpec as P

NEAR = 4
NEWTON_STEPS = 10
BF16 = jnp.bfloat16
F32 = jnp.float32
VMEM_LIMIT = 48 << 20


def split(x):
    high = x.astype(BF16)
    return high, (x - high.astype(F32)).astype(BF16)


def dot(left, right):
    return jnp.dot(left, right, preferred_element_type=F32)


def product(left, right):
    return dot(left[0], right[0]) + (dot(left[0], right[1]) + dot(left[1], right[0]))


def stacked_product(left, right):
    rows = left[0].shape[0]
    both = dot(jnp.concatenate(left, axis=0), right[0])
    return both[:rows] + (both[rows:] + dot(left[0], right[1]))


def identity(size):
    rows = lax.broadcasted_iota(jnp.int32, (size, size), 0)
    columns = lax.broadcasted_iota(jnp.int32, (size, size), 1)
    return (rows == columns).astype(F32)


def normalized(gram):
    scale = jnp.sqrt(jnp.sum(gram * gram)) + 1e-06
    return gram / scale, jnp.sqrt(scale)


def newton_batch(grams):
    eye = identity(grams[0].shape[0])
    count = range(len(grams))
    scaled = [normalized(gram) for gram in grams]
    power = [approx for approx, _ in scaled]
    start = [split(approx) for approx in power]
    parts = list(start)
    inverse = None
    for pair in range(NEWTON_STEPS // 2):
        square = [product(p, p) for p in parts]
        square_parts = [split(p) for p in square]
        tail = [split(0.0625 * square[i] - 0.5625 * power[i]) for i in count]
        factor = [
            (2.25 * eye + (1.6875 * square[i] - 2.4375 * power[i]))
            + product(tail[i], square_parts[i])
            for i in count
        ]
        factor_parts = [split(q) for q in factor]
        if pair < NEWTON_STEPS // 2 - 1:
            twice = [split(product(q, q)) for q in factor_parts]
            power = [product(twice[i], parts[i]) for i in count]
            parts = [split(p) for p in power]
        if inverse is None:
            inverse = factor
            inverse_parts = factor_parts
        else:
            inverse = [product(inverse_parts[i], factor_parts[i]) for i in count]
            inverse_parts = [split(y) for y in inverse]
    basis = [inverse[i] / scaled[i][1] for i in count]
    root = [product(inverse_parts[i], start[i]) * scaled[i][1] for i in count]
    return basis, root


def newton_single(gram, beside=None):
    size = gram.shape[0]
    half = size // 2
    blocks = [slice(0, half), slice(half, size)]
    power, root_scale = normalized(gram)
    start = split(power)
    parts = start
    inverse = None
    for step in range(NEWTON_STEPS):
        if step < NEWTON_STEPS - 1:
            first = [
                1.5 * power[rows]
                - 0.5 * stacked_product((parts[0][rows], parts[1][rows]), parts)
                for rows in blocks
            ]
        if beside is not None:
            beside(step)
        if step < NEWTON_STEPS - 1:
            following = jnp.concatenate(
                [1.5 * u - 0.5 * stacked_product(split(u), parts) for u in first], axis=0
            )
        if inverse is None:
            inverse = 1.5 * identity(size) - 0.5 * power
        else:
            inverse = jnp.concatenate(
                [
                    1.5 * inverse[rows]
                    - 0.5
                    * stacked_product((inverse_parts[0][rows], inverse_parts[1][rows]), parts)
                    for rows in blocks
                ],
                axis=0,
            )
        inverse_parts = split(inverse)
        if step < NEWTON_STEPS - 1:
            power = following
            parts = split(power)
    root = jnp.concatenate(
        [
            stacked_product((inverse_parts[0][rows], inverse_parts[1][rows]), start)
            for rows in blocks
        ],
        axis=0,
    )
    return inverse / root_scale, root * root_scale


def sibling_gram(low, high):
    low, high = split(low), split(high)
    return product(low, low) + product(high, high)


def packed(factor):
    half = factor.shape[0] // 2
    return jnp.concatenate([factor[:half, :half], factor[:half, half:], factor[half:, half:]], axis=0)


def unpacked(blocks):
    half = blocks.shape[1]
    first, cross, second = blocks[:half], blocks[half : 2 * half], blocks[2 * half :]
    upper = jnp.concatenate([first, cross], axis=1)
    return jnp.concatenate([upper, jnp.concatenate([cross.T, second], axis=1)], axis=0)


def edge_column(meta, leaves, index):
    column = meta[index]
    outside = jnp.logical_or(column < 0, column >= 2 * leaves)
    return outside, jnp.where(column < 0, column + NEAR, column - 2 * leaves)


def edge_leaf(meta, leaves, per_leaf, place):
    return jnp.where(meta[leaves * per_leaf] == 0, place, leaves - 1 - place)


def edge_plan(meta, leaves, per_leaf):
    plan = []
    beyond = jnp.int32(0)
    for place in range(leaves):
        leaf = edge_leaf(meta, leaves, per_leaf, place)
        most = leaves - place
        found = jnp.int32(0)
        slots = [jnp.int32(0)] * most
        columns = [jnp.int32(NEAR)] * most
        for slot in range(1, per_leaf):
            outside, column = edge_column(meta, leaves, leaf * per_leaf + slot)
            for item in range(most):
                hit = jnp.logical_and(outside, found == item)
                slots[item] = jnp.where(hit, slot, slots[item])
                columns[item] = jnp.where(hit, column, columns[item])
            found = found + outside.astype(jnp.int32)
        beyond = beyond + jnp.maximum(found - most, 0)
        plan.append((leaf, slots, columns))
    return plan, beyond


def inside_sum(
    meta, near, mine, sister, out, edge_blocks, window, held, sems, edge_sems, window_sems
):
    leaves, per_leaf = near.shape[0], near.shape[1]

    def inside(index):
        column = meta[index]
        return jnp.logical_and(column >= 0, column < 2 * leaves)

    def fetch(index):
        return pltpu.make_async_copy(
            near.at[index // per_leaf, index % per_leaf], held.at[index], sems.at[index]
        )

    core = meta[leaves * per_leaf]
    halves = [
        pltpu.make_async_copy(rows, window.at[pl.ds(place * leaves, leaves)], window_sems.at[number])
        for number, (rows, place) in enumerate(((mine, core), (sister, 1 - core)))
    ]
    for copy in halves:
        copy.start()
    for index in range(leaves * per_leaf):
        pl.when(inside(index))(fetch(index).start)
    plan, _ = edge_plan(meta, leaves, per_leaf)
    copies = []
    for leaf, slots, _ in plan:
        for slot in slots:
            index = len(copies)
            copies.append(
                pltpu.make_async_copy(
                    near.at[leaf, slot], edge_blocks.at[index], edge_sems.at[index]
                )
            )
            copies[-1].start()
    for copy in halves:
        copy.wait()

    def leaf_body(leaf, carry):
        base = leaf * per_leaf
        pltpu.make_async_copy(near.at[leaf, 0], held.at[base], sems.at[base]).wait()
        out[leaf] = dot(held[base], window[meta[base]])

        def block_body(slot, inner):
            index = base + slot

            @pl.when(inside(index))
            def _():
                pltpu.make_async_copy(
                    near.at[leaf, slot], held.at[index], sems.at[index]
                ).wait()
                out[leaf] += dot(held[index], window[meta[index]])

            return inner

        return lax.fori_loop(1, per_leaf, block_body, carry)

    lax.fori_loop(0, leaves, leaf_body, 0)
    for copy in copies:
        copy.wait()


def leaf_stage(
    meta, outer, partial, edge_blocks, near, bases, transfers, top, spare, sums, basis, merged, spare_sem, out_sems
):
    leaves, per_leaf = near.shape[0], near.shape[1]
    rank = partial.shape[2]
    half = partial.shape[1] // 2
    plan, beyond = edge_plan(meta, leaves, per_leaf)
    index = 0
    for leaf, _, columns in plan:
        blocks = [edge_blocks[index + item] for item in range(len(columns))]
        index += len(columns)
        windows = []
        for column in columns:
            window = outer[jnp.minimum(column, NEAR - 1)]
            windows.append(jnp.where(column < NEAR, window, jnp.zeros_like(window)))
        sums[leaf] = partial[leaf] + dot(
            jnp.concatenate(blocks, axis=1), jnp.concatenate(windows, axis=0)
        )

    @pl.when(beyond > 0)
    def _():
        def body(item, found):
            place, slot = item // (per_leaf - 1), 1 + item % (per_leaf - 1)
            leaf = edge_leaf(meta, leaves, per_leaf, place)
            found = jnp.where(slot == 1, 0, found)
            outside, column = edge_column(meta, leaves, leaf * per_leaf + slot)

            @pl.when(jnp.logical_and(outside, found >= leaves - place))
            def _():
                copy = pltpu.make_async_copy(near.at[leaf, slot], spare, spare_sem)
                copy.start()
                copy.wait()
                sums[leaf] += dot(spare[...], outer[column])

            return found + outside.astype(jnp.int32)

        lax.fori_loop(0, leaves * (per_leaf - 1), body, jnp.int32(0))

    grams = []
    for leaf in range(leaves):
        high, low = split(sums[leaf])
        turned = high.T
        cross = dot(turned, low)
        grams.append(dot(turned, high) + (cross + cross.T))
    inverse, factors = newton_batch(grams)

    later = []

    def leaf_basis(leaf, inverse_parts, part):
        rows = slice(part * half, (part + 1) * half)
        basis[leaf, rows] = product(split(sums[leaf, rows]), inverse_parts)
        if part == 1:
            pltpu.make_async_copy(basis.at[leaf], bases.at[leaf], out_sems.at[leaf]).start()

    def node_basis(slot, factor, inverse_parts, part):
        rows = slice(part * rank, (part + 1) * rank)
        merged[slot - 1, rows] = product(split(factor), inverse_parts)
        if part == 1:
            pltpu.make_async_copy(
                merged.at[slot - 1], transfers.at[slot], out_sems.at[leaves + slot - 1]
            ).start()

    for leaf in range(leaves):
        inverse_parts = split(inverse[leaf])
        for part in range(2):
            later.append((leaf_basis, leaf, inverse_parts, part))
    span = 1
    while len(factors) > 1:
        grams = [
            sibling_gram(factors[2 * node], factors[2 * node + 1])
            for node in range(len(factors) // 2)
        ]
        if len(grams) > 1:
            inverse, parents = newton_batch(grams)
        else:
            each = -(-len(later) // (NEWTON_STEPS - 1))

            def beside(step):
                for call, *arguments in later[step * each : (step + 1) * each]:
                    call(*arguments)

            single, parent = newton_single(grams[0], beside)
            inverse, parents = [single], [parent]
            top[...] = packed(parent)
            later = []
        for node in range(len(grams)):
            slot = node * 2 * span + span
            inverse_parts = split(inverse[node])
            for part in range(2):
                later.append((node_basis, slot, factors[2 * node + part], inverse_parts, part))
        factors = parents
        span *= 2
    for call, *arguments in later:
        call(*arguments)
    for leaf in range(leaves):
        pltpu.make_async_copy(basis.at[leaf], bases.at[leaf], out_sems.at[leaf]).wait()
    for slot in range(1, leaves):
        pltpu.make_async_copy(
            merged.at[slot - 1], transfers.at[slot], out_sems.at[leaves + slot - 1]
        ).wait()


def merge_stage(pair, factor, inverse):
    inverse[...], root = newton_single(sibling_gram(unpacked(pair[0]), unpacked(pair[1])))
    factor[...] = packed(root)


def root_stage(scale, levels, meta, pair, *refs):
    pairs, inverses = refs[: levels - 1], refs[levels - 1 : 2 * levels - 2]
    transfers_in, transfers, root, own_pair, own_inverse, merged, sems = refs[2 * levels - 2 :]
    del transfers_in
    rank = root.shape[0]
    level = meta[0]

    def each_level(action):
        for number in range(1, levels):

            @pl.when(level == number)
            def _():
                for copy in (
                    pltpu.make_async_copy(pairs[number - 1], own_pair, sems.at[0]),
                    pltpu.make_async_copy(inverses[number - 1], own_inverse, sems.at[1]),
                ):
                    action(copy)

    def node_basis(part, inverse_parts):
        rows = slice(part * rank, (part + 1) * rank)
        merged[rows] = product(split(unpacked(own_pair[part])), inverse_parts)

    each_level(lambda copy: copy.start())

    @pl.when(jnp.logical_or(level == 0, level == levels))
    def _():
        own_pair[...] = pair[...]
        own_inverse[...] = jnp.zeros_like(own_inverse)

    def beside(step):
        if step == NEWTON_STEPS // 2:
            each_level(lambda copy: copy.wait())
        if NEWTON_STEPS // 2 <= step < NEWTON_STEPS // 2 + 2:
            node_basis(step - NEWTON_STEPS // 2, split(own_inverse[...]))

    inverse, factor = newton_single(sibling_gram(unpacked(pair[0]), unpacked(pair[1])), beside)
    root[...] = factor * scale

    @pl.when(level == levels)
    def _():
        for part in range(2):
            node_basis(part, split(inverse))

    out = pltpu.make_async_copy(merged, transfers.at[0], sems.at[2])
    out.start()
    out.wait()


def spec(space):
    return pl.BlockSpec(memory_space=space)


def params():
    return pltpu.CompilerParams(vmem_limit_bytes=VMEM_LIMIT)


def dev_groups(size, bit):
    flip = {0: 1, 1: 2, 2: 6, 3: 8, 4: 24}.get(bit, 1 << bit)
    return [[i, i ^ flip] for i in range(size) if i & (1 << bit) == 0]


def local(near_blocks, samples, pattern):
    leaves, per_leaf, leaf_size = near_blocks.shape[:3]
    rank = samples.shape[1]
    grp_count, dev_count = lax.axis_size("grp"), lax.axis_size("dev")
    devices = grp_count * dev_count
    device = lax.axis_index("grp") * dev_count + lax.axis_index("dev")
    chip, core = device // 2, device % 2
    edge = [(i, i + 1) for i in range(1, devices - 1, 2)]
    edge += [(j, i) for i, j in edge]
    outer = lax.ppermute(samples, ("grp", "dev"), edge)
    sister = lax.ppermute(samples, "dev", [(i, i ^ 1) for i in range(dev_count)])
    mine = samples.reshape(leaves, leaf_size, rank)
    sister = sister.reshape(leaves, leaf_size, rank)
    outer = outer.reshape(leaves, leaf_size, rank)

    own = core * leaves + jnp.arange(leaves, dtype=jnp.int32)[:, None]
    columns = jnp.concatenate([own, pattern - chip * 2 * leaves], axis=1).reshape(-1)
    meta = jnp.concatenate([columns, core[None].astype(jnp.int32)])

    leaf_sums = jax.ShapeDtypeStruct((leaves, leaf_size, rank), F32)
    blocks = leaves * per_leaf
    edges = leaves * (leaves + 1) // 2
    partial, edge_blocks = pl.pallas_call(
        inside_sum,
        out_shape=[leaf_sums, jax.ShapeDtypeStruct((edges, leaf_size, leaf_size), BF16)],
        in_specs=[spec(pltpu.SMEM)] + [spec(pl.ANY)] * 3,
        out_specs=[spec(pltpu.VMEM)] * 2,
        scratch_shapes=[
            pltpu.VMEM((2 * leaves, leaf_size, rank), BF16),
            pltpu.VMEM((blocks, leaf_size, leaf_size), BF16),
            pltpu.SemaphoreType.DMA((blocks,)),
            pltpu.SemaphoreType.DMA((edges,)),
            pltpu.SemaphoreType.DMA((2,)),
        ],
        compiler_params=params(),
        cost_estimate=pl.CostEstimate(
            flops=2 * blocks * leaf_size * leaf_size * rank,
            bytes_accessed=2 * blocks * leaf_size * leaf_size,
            transcendentals=0,
        ),
        name="inside_sum",
    )(meta, near_blocks, mine, sister)

    square = jax.ShapeDtypeStruct((rank, rank), F32)
    half = rank // 2
    upper = jax.ShapeDtypeStruct((3 * half, half), F32)
    bases, transfers, factor = pl.pallas_call(
        leaf_stage,
        out_shape=[leaf_sums, jax.ShapeDtypeStruct((leaves, 2 * rank, rank), F32), upper],
        in_specs=[spec(pltpu.SMEM)] + [spec(pltpu.VMEM)] * 3 + [spec(pl.ANY)],
        out_specs=[spec(pl.ANY), spec(pl.ANY), spec(pltpu.VMEM)],
        scratch_shapes=[
            pltpu.VMEM((leaf_size, leaf_size), BF16),
            pltpu.VMEM((leaves, leaf_size, rank), F32),
            pltpu.VMEM((leaves, leaf_size, rank), F32),
            pltpu.VMEM((leaves - 1, 2 * rank, rank), F32),
            pltpu.SemaphoreType.DMA,
            pltpu.SemaphoreType.DMA((2 * leaves - 1,)),
        ],
        compiler_params=params(),
        name="leaf_stage",
    )(meta, outer, partial, edge_blocks, near_blocks)

    dev_bits = dev_count.bit_length() - 1
    grp_bits = grp_count.bit_length() - 1
    groups = [("dev", dev_groups(dev_count, bit)) for bit in range(dev_bits)]
    flips = [1, 3]
    groups += [
        ("grp", [[i, i ^ flips[bit]] for i in range(grp_count) if i & (1 << bit) == 0])
        for bit in range(grp_bits)
    ]
    levels = len(groups)
    pairs, inverses = [], []
    for number, (axis, members) in enumerate(groups):
        pair = lax.all_gather(factor, axis, axis_index_groups=members)
        pairs.append(pair)
        if number < levels - 1:
            factor, inverse = pl.pallas_call(
                merge_stage,
                out_shape=[upper, square],
                in_specs=[spec(pltpu.VMEM)],
                out_specs=[spec(pltpu.VMEM), spec(pltpu.VMEM)],
                compiler_params=params(),
                name="merge_stage",
            )(pair)
            inverses.append(inverse)

    owned = jnp.int32(0)
    for number in range(1, levels + 1):
        is_owner = device & ((1 << number) - 1) == 1 << (number - 1)
        owned = jnp.where(is_owner, number, owned)
    total_rows = leaves * leaf_size * devices

    def root_body(*refs):
        root_stage(1.0 / math.sqrt(total_rows), levels, *refs)

    transfers, root = pl.pallas_call(
        root_body,
        out_shape=[jax.ShapeDtypeStruct((leaves, 2 * rank, rank), F32), square],
        in_specs=[spec(pltpu.SMEM), spec(pltpu.VMEM)] + [spec(pl.ANY)] * (2 * levels - 1),
        out_specs=[spec(pl.ANY), spec(pltpu.VMEM)],
        scratch_shapes=[
            pltpu.VMEM((2, 3 * half, half), F32),
            pltpu.VMEM((rank, rank), F32),
            pltpu.VMEM((2 * rank, rank), F32),
            pltpu.SemaphoreType.DMA((3,)),
        ],
        input_output_aliases={2 * levels: 0},
        compiler_params=params(),
        name="root_stage",
    )(owned[None], pairs[-1], *pairs[:-1], *inverses, transfers)
    return (bases.reshape(leaves * leaf_size, rank), transfers, root)


def solution(mesh):
    in_specs = (
        P(("grp", "dev"), None, None, None),
        P(("grp", "dev"), None),
        P(("grp", "dev"), None),
    )
    out_specs = (P(("grp", "dev"), None), P(("grp", "dev"), None, None), P())
    return jax.shard_map(local, mesh=mesh, in_specs=in_specs, out_specs=out_specs, check_vma=False)
```

```python
import math

import jax
import jax.numpy as jnp
from jax import lax
from jax.experimental import pallas as pl
from jax.experimental.pallas import tpu as pltpu
from jax.sharding import PartitionSpec as P

NEAR = 4
NEWTON_STEPS = 10
BF16 = jnp.bfloat16
F32 = jnp.float32
MIB = 1 << 20


def split(x):
    high = x.astype(BF16)
    return high, (x - high.astype(F32)).astype(BF16)


def dot(left, right):
    return jnp.dot(left, right, preferred_element_type=F32)


def product(left, right):
    return dot(left[0], right[0]) + (dot(left[0], right[1]) + dot(left[1], right[0]))


def stacked_product(left, right):
    rows = left[0].shape[0]
    both = dot(jnp.concatenate(left, axis=0), right[0])
    return both[:rows] + (both[rows:] + dot(left[0], right[1]))


def identity(size):
    rows = lax.broadcasted_iota(jnp.int32, (size, size), 0)
    columns = lax.broadcasted_iota(jnp.int32, (size, size), 1)
    return (rows == columns).astype(F32)


def normalized(gram):
    scale = jnp.sqrt(jnp.sum(gram * gram)) + 1e-06
    return gram / scale, jnp.sqrt(scale)


def newton_batch(grams):
    eye = identity(grams[0].shape[0])
    count = range(len(grams))
    scaled = [normalized(gram) for gram in grams]
    power = [approx for approx, _ in scaled]
    start = [split(approx) for approx in power]
    parts = list(start)
    inverse = None
    for pair in range(NEWTON_STEPS // 2):
        square = [product(p, p) for p in parts]
        square_parts = [split(p) for p in square]
        tail = [split(0.0625 * square[i] - 0.5625 * power[i]) for i in count]
        factor = [
            (2.25 * eye + (1.6875 * square[i] - 2.4375 * power[i]))
            + product(tail[i], square_parts[i])
            for i in count
        ]
        factor_parts = [split(q) for q in factor]
        if pair < NEWTON_STEPS // 2 - 1:
            twice = [split(product(q, q)) for q in factor_parts]
            power = [product(twice[i], parts[i]) for i in count]
            parts = [split(p) for p in power]
        if inverse is None:
            inverse = factor
            inverse_parts = factor_parts
        else:
            inverse = [product(inverse_parts[i], factor_parts[i]) for i in count]
            inverse_parts = [split(y) for y in inverse]
    basis = [inverse[i] / scaled[i][1] for i in count]
    root = [product(inverse_parts[i], start[i]) * scaled[i][1] for i in count]
    return basis, root


def newton_single(gram, beside=None):
    size = gram.shape[0]
    half = size // 2
    blocks = [slice(0, half), slice(half, size)]
    power, root_scale = normalized(gram)
    start = split(power)
    parts = start
    inverse = None
    for step in range(NEWTON_STEPS):
        if step < NEWTON_STEPS - 1:
            first = [
                1.5 * power[rows]
                - 0.5 * stacked_product((parts[0][rows], parts[1][rows]), parts)
                for rows in blocks
            ]
        if beside is not None:
            beside(step)
        if step < NEWTON_STEPS - 1:
            following = jnp.concatenate(
                [1.5 * u - 0.5 * stacked_product(split(u), parts) for u in first], axis=0
            )
        if inverse is None:
            inverse = 1.5 * identity(size) - 0.5 * power
        else:
            inverse = jnp.concatenate(
                [
                    1.5 * inverse[rows]
                    - 0.5
                    * stacked_product((inverse_parts[0][rows], inverse_parts[1][rows]), parts)
                    for rows in blocks
                ],
                axis=0,
            )
        inverse_parts = split(inverse)
        if step < NEWTON_STEPS - 1:
            power = following
            parts = split(power)
    root = jnp.concatenate(
        [
            stacked_product((inverse_parts[0][rows], inverse_parts[1][rows]), start)
            for rows in blocks
        ],
        axis=0,
    )
    return inverse / root_scale, root * root_scale


def sibling_gram(low, high):
    low, high = split(low), split(high)
    return product(low, low) + product(high, high)


def packed(factor):
    half = factor.shape[0] // 2
    return jnp.concatenate([factor[:half, :half], factor[:half, half:], factor[half:, half:]], axis=0)


def unpacked(blocks):
    half = blocks.shape[1]
    first, cross, second = blocks[:half], blocks[half : 2 * half], blocks[2 * half :]
    upper = jnp.concatenate([first, cross], axis=1)
    return jnp.concatenate([upper, jnp.concatenate([cross.T, second], axis=1)], axis=0)


def edge_column(meta, leaves, index):
    column = meta[index]
    outside = jnp.logical_or(column < 0, column >= 2 * leaves)
    return outside, jnp.where(column < 0, column + NEAR, column - 2 * leaves)


def edge_leaf(meta, leaves, per_leaf, place):
    return jnp.where(meta[leaves * per_leaf] == 0, place, leaves - 1 - place)


def edge_plan(meta, leaves, per_leaf):
    plan = []
    beyond = jnp.int32(0)
    for place in range(leaves):
        leaf = edge_leaf(meta, leaves, per_leaf, place)
        most = leaves - place
        found = jnp.int32(0)
        slots = [jnp.int32(0)] * most
        columns = [jnp.int32(NEAR)] * most
        for slot in range(1, per_leaf):
            outside, column = edge_column(meta, leaves, leaf * per_leaf + slot)
            for item in range(most):
                hit = jnp.logical_and(outside, found == item)
                slots[item] = jnp.where(hit, slot, slots[item])
                columns[item] = jnp.where(hit, column, columns[item])
            found = found + outside.astype(jnp.int32)
        beyond = beyond + jnp.maximum(found - most, 0)
        plan.append((leaf, slots, columns))
    return plan, beyond


def inside_sum(
    meta, near, mine, sister, out, edge_blocks, window, held, sems, edge_sems, window_sems
):
    leaves, per_leaf = near.shape[0], near.shape[1]

    def inside(index):
        column = meta[index]
        return jnp.logical_and(column >= 0, column < 2 * leaves)

    def fetch(index):
        return pltpu.make_async_copy(
            near.at[index // per_leaf, index % per_leaf], held.at[index], sems.at[index]
        )

    core = meta[leaves * per_leaf]
    halves = [
        pltpu.make_async_copy(rows, window.at[pl.ds(place * leaves, leaves)], window_sems.at[number])
        for number, (rows, place) in enumerate(((mine, core), (sister, 1 - core)))
    ]
    for copy in halves:
        copy.start()
    for index in range(leaves * per_leaf):
        pl.when(inside(index))(fetch(index).start)
    plan, _ = edge_plan(meta, leaves, per_leaf)
    copies = []
    for leaf, slots, _ in plan:
        for slot in slots:
            index = len(copies)
            copies.append(
                pltpu.make_async_copy(
                    near.at[leaf, slot], edge_blocks.at[index], edge_sems.at[index]
                )
            )
            copies[-1].start()
    for copy in halves:
        copy.wait()

    def leaf_body(leaf, carry):
        base = leaf * per_leaf
        pltpu.make_async_copy(near.at[leaf, 0], held.at[base], sems.at[base]).wait()
        out[leaf] = dot(held[base], window[meta[base]])

        def block_body(slot, inner):
            index = base + slot

            @pl.when(inside(index))
            def _():
                pltpu.make_async_copy(
                    near.at[leaf, slot], held.at[index], sems.at[index]
                ).wait()
                out[leaf] += dot(held[index], window[meta[index]])

            return inner

        return lax.fori_loop(1, per_leaf, block_body, carry)

    lax.fori_loop(0, leaves, leaf_body, 0)
    for copy in copies:
        copy.wait()


def leaf_stage(
    meta, outer, partial, edge_blocks, near, bases, transfers, top, spare, sums, basis, merged, spare_sem, out_sems
):
    leaves, per_leaf = near.shape[0], near.shape[1]
    rank = partial.shape[2]
    half = partial.shape[1] // 2
    plan, beyond = edge_plan(meta, leaves, per_leaf)
    index = 0
    for leaf, _, columns in plan:
        blocks = [edge_blocks[index + item] for item in range(len(columns))]
        index += len(columns)
        windows = []
        for column in columns:
            window = outer[jnp.minimum(column, NEAR - 1)]
            windows.append(jnp.where(column < NEAR, window, jnp.zeros_like(window)))
        sums[leaf] = partial[leaf] + dot(
            jnp.concatenate(blocks, axis=1), jnp.concatenate(windows, axis=0)
        )

    @pl.when(beyond > 0)
    def _():
        def body(item, found):
            place, slot = item // (per_leaf - 1), 1 + item % (per_leaf - 1)
            leaf = edge_leaf(meta, leaves, per_leaf, place)
            found = jnp.where(slot == 1, 0, found)
            outside, column = edge_column(meta, leaves, leaf * per_leaf + slot)

            @pl.when(jnp.logical_and(outside, found >= leaves - place))
            def _():
                copy = pltpu.make_async_copy(near.at[leaf, slot], spare, spare_sem)
                copy.start()
                copy.wait()
                sums[leaf] += dot(spare[...], outer[column])

            return found + outside.astype(jnp.int32)

        lax.fori_loop(0, leaves * (per_leaf - 1), body, jnp.int32(0))

    grams = []
    for leaf in range(leaves):
        high, low = split(sums[leaf])
        turned = high.T
        cross = dot(turned, low)
        grams.append(dot(turned, high) + (cross + cross.T))
    inverse, factors = newton_batch(grams)

    later = []

    def leaf_basis(leaf, inverse_parts, part):
        rows = slice(part * half, (part + 1) * half)
        basis[leaf, rows] = product(split(sums[leaf, rows]), inverse_parts)
        if part == 1:
            pltpu.make_async_copy(basis.at[leaf], bases.at[leaf], out_sems.at[leaf]).start()

    def node_basis(slot, factor, inverse_parts, part):
        rows = slice(part * rank, (part + 1) * rank)
        merged[slot - 1, rows] = product(split(factor), inverse_parts)
        if part == 1:
            pltpu.make_async_copy(
                merged.at[slot - 1], transfers.at[slot], out_sems.at[leaves + slot - 1]
            ).start()

    for leaf in range(leaves):
        inverse_parts = split(inverse[leaf])
        for part in range(2):
            later.append((leaf_basis, leaf, inverse_parts, part))
    span = 1
    while len(factors) > 1:
        grams = [
            sibling_gram(factors[2 * node], factors[2 * node + 1])
            for node in range(len(factors) // 2)
        ]
        if len(grams) > 1:
            inverse, parents = newton_batch(grams)
        else:
            each = -(-len(later) // (NEWTON_STEPS - 1))

            def beside(step):
                for call, *arguments in later[step * each : (step + 1) * each]:
                    call(*arguments)

            single, parent = newton_single(grams[0], beside)
            inverse, parents = [single], [parent]
            top[...] = packed(parent)
            later = []
        for node in range(len(grams)):
            slot = node * 2 * span + span
            inverse_parts = split(inverse[node])
            for part in range(2):
                later.append((node_basis, slot, factors[2 * node + part], inverse_parts, part))
        factors = parents
        span *= 2
    for call, *arguments in later:
        call(*arguments)
    for leaf in range(leaves):
        pltpu.make_async_copy(basis.at[leaf], bases.at[leaf], out_sems.at[leaf]).wait()
    for slot in range(1, leaves):
        pltpu.make_async_copy(
            merged.at[slot - 1], transfers.at[slot], out_sems.at[leaves + slot - 1]
        ).wait()


def merge_stage(core, pair, factor, inverse):
    inverse[...], root = newton_single(sibling_gram(unpacked(pair[0]), unpacked(pair[1])))
    blocks = packed(root)
    half = blocks.shape[0] // 2
    factor[...] = jnp.where(core[0] == 0, blocks[:half], blocks[half:])


def root_stage(scale, levels, meta, pair, *refs):
    pairs, inverses = refs[: levels - 1], refs[levels - 1 : 2 * levels - 2]
    transfers_in, transfers, root, own_pair, own_inverse, merged, sems = refs[2 * levels - 2 :]
    del transfers_in
    rank = root.shape[0]
    level = meta[0]
    fetched = jnp.where(jnp.logical_or(level == 0, level == levels), 1, level)

    def fetches(number):
        return (
            pltpu.make_async_copy(pairs[number - 1], own_pair, sems.at[0]),
            pltpu.make_async_copy(inverses[number - 1], own_inverse, sems.at[1]),
        )

    def node_basis(blocks, inverse_parts, part):
        rows = slice(part * rank, (part + 1) * rank)
        merged[rows] = product(split(unpacked(blocks)), inverse_parts)

    for number in range(1, levels):

        @pl.when(fetched == number)
        def _():
            for copy in fetches(number):
                copy.start()

    store = pltpu.make_async_copy(merged, transfers.at[0], sems.at[2])

    def beside(step):
        if step == 4:
            for copy in fetches(1):
                copy.wait()
        if step in (5, 6):
            own = own_inverse[...]
            own = jnp.where(level > 0, own, jnp.zeros_like(own))
            node_basis(own_pair[step - 5], split(own), step - 5)
        if step == 7:
            pl.when(level < levels)(store.start)

    inverse, factor = newton_single(sibling_gram(unpacked(pair[0]), unpacked(pair[1])), beside)
    root[...] = factor * scale

    @pl.when(level == levels)
    def _():
        for part in range(2):
            node_basis(pair[part], split(inverse), part)
        store.start()

    store.wait()


def spec(space):
    return pl.BlockSpec(memory_space=space)


def params(size):
    return pltpu.CompilerParams(vmem_limit_bytes=size * MIB)


def chip_groups(chips, bit):
    flip = (3 if bit % 2 else 1) << (bit - bit % 2)
    pairs = [(i, i ^ flip) for i in range(chips) if i & (1 << bit) == 0]
    return [[2 * i, 2 * i + 1, 2 * j, 2 * j + 1] for i, j in pairs]


def local(near_blocks, samples, pattern):
    leaves, per_leaf, leaf_size = near_blocks.shape[:3]
    rank = samples.shape[1]
    grp_count, dev_count = lax.axis_size("grp"), lax.axis_size("dev")
    devices = grp_count * dev_count
    device = lax.axis_index("grp") * dev_count + lax.axis_index("dev")
    chip, core = device // 2, device % 2
    edge = [(i, i + 1) for i in range(1, devices - 1, 2)]
    edge += [(j, i) for i, j in edge]
    outer = lax.ppermute(samples, ("grp", "dev"), edge)
    sister = lax.ppermute(samples, "dev", [(i, i ^ 1) for i in range(dev_count)])
    mine = samples.reshape(leaves, leaf_size, rank)
    sister = sister.reshape(leaves, leaf_size, rank)
    outer = outer.reshape(leaves, leaf_size, rank)

    own = core * leaves + jnp.arange(leaves, dtype=jnp.int32)[:, None]
    columns = jnp.concatenate([own, pattern - chip * 2 * leaves], axis=1).reshape(-1)
    meta = jnp.concatenate([columns, core[None].astype(jnp.int32)])

    leaf_sums = jax.ShapeDtypeStruct((leaves, leaf_size, rank), F32)
    blocks = leaves * per_leaf
    edges = leaves * (leaves + 1) // 2
    partial, edge_blocks = pl.pallas_call(
        inside_sum,
        out_shape=[leaf_sums, jax.ShapeDtypeStruct((edges, leaf_size, leaf_size), BF16)],
        in_specs=[spec(pltpu.SMEM)] + [spec(pl.ANY)] * 3,
        out_specs=[spec(pltpu.VMEM)] * 2,
        scratch_shapes=[
            pltpu.VMEM((2 * leaves, leaf_size, rank), BF16),
            pltpu.VMEM((blocks, leaf_size, leaf_size), BF16),
            pltpu.SemaphoreType.DMA((blocks,)),
            pltpu.SemaphoreType.DMA((edges,)),
            pltpu.SemaphoreType.DMA((2,)),
        ],
        compiler_params=params(18),
        cost_estimate=pl.CostEstimate(
            flops=2 * blocks * leaf_size * leaf_size * rank,
            bytes_accessed=2 * blocks * leaf_size * leaf_size,
            transcendentals=0,
        ),
        name="inside_sum",
    )(meta, near_blocks, mine, sister)

    square = jax.ShapeDtypeStruct((rank, rank), F32)
    half = rank // 2
    upper = jax.ShapeDtypeStruct((3 * half, half), F32)
    bases, transfers, factor = pl.pallas_call(
        leaf_stage,
        out_shape=[leaf_sums, jax.ShapeDtypeStruct((leaves, 2 * rank, rank), F32), upper],
        in_specs=[spec(pltpu.SMEM)] + [spec(pltpu.VMEM)] * 3 + [spec(pl.ANY)],
        out_specs=[spec(pl.ANY), spec(pl.ANY), spec(pltpu.VMEM)],
        scratch_shapes=[
            pltpu.VMEM((leaf_size, leaf_size), BF16),
            pltpu.VMEM((leaves, leaf_size, rank), F32),
            pltpu.VMEM((leaves, leaf_size, rank), F32),
            pltpu.VMEM((leaves - 1, 2 * rank, rank), F32),
            pltpu.SemaphoreType.DMA,
            pltpu.SemaphoreType.DMA((2 * leaves - 1,)),
        ],
        compiler_params=params(30),
        name="leaf_stage",
    )(meta, outer, partial, edge_blocks, near_blocks)

    levels = devices.bit_length() - 1
    core_meta = core[None].astype(jnp.int32)
    pairs, inverses = [], []
    for number in range(levels):
        if number == 0:
            members = [[i, i + 1] for i in range(0, devices, 2)]
        else:
            members = chip_groups(devices // 2, number - 1)
        pair = lax.all_gather(factor, ("grp", "dev"), axis_index_groups=members)
        pair = pair.reshape(2, 3 * half, half)
        pairs.append(pair)
        if number < levels - 1:
            factor, inverse = pl.pallas_call(
                merge_stage,
                out_shape=[jax.ShapeDtypeStruct((3 * half // 2, half), F32), square],
                in_specs=[spec(pltpu.SMEM), spec(pltpu.VMEM)],
                out_specs=[spec(pltpu.VMEM), spec(pltpu.VMEM)],
                compiler_params=params(12),
                name="merge_stage",
            )(core_meta, pair)
            inverses.append(inverse)

    owned = jnp.int32(0)
    for number in range(1, levels + 1):
        is_owner = device & ((1 << number) - 1) == 1 << (number - 1)
        owned = jnp.where(is_owner, number, owned)
    total_rows = leaves * leaf_size * devices

    def root_body(*refs):
        root_stage(1.0 / math.sqrt(total_rows), levels, *refs)

    transfers, root = pl.pallas_call(
        root_body,
        out_shape=[jax.ShapeDtypeStruct((leaves, 2 * rank, rank), F32), square],
        in_specs=[spec(pltpu.SMEM), spec(pltpu.VMEM)] + [spec(pl.ANY)] * (2 * levels - 1),
        out_specs=[spec(pl.ANY), spec(pltpu.VMEM)],
        scratch_shapes=[
            pltpu.VMEM((2, 3 * half, half), F32),
            pltpu.VMEM((rank, rank), F32),
            pltpu.VMEM((2 * rank, rank), F32),
            pltpu.SemaphoreType.DMA((3,)),
        ],
        input_output_aliases={2 * levels: 0},
        compiler_params=params(14),
        name="root_stage",
    )(owned[None], pairs[-1], *pairs[:-1], *inverses, transfers)
    return (bases.reshape(leaves * leaf_size, rank), transfers, root)


def solution(mesh):
    in_specs = (
        P(("grp", "dev"), None, None, None),
        P(("grp", "dev"), None),
        P(("grp", "dev"), None),
    )
    out_specs = (P(("grp", "dev"), None), P(("grp", "dev"), None, None), P())
    return jax.shard_map(local, mesh=mesh, in_specs=in_specs, out_specs=out_specs, check_vma=False)
```

```python
import math

import jax
import jax.numpy as jnp
from jax import lax
from jax.experimental import pallas as pl
from jax.experimental.pallas import tpu as pltpu
from jax.sharding import PartitionSpec as P

NEAR = 4
NEWTON_STEPS = 10
BF16 = jnp.bfloat16
F32 = jnp.float32
MIB = 1 << 20


def split(x):
    high = x.astype(BF16)
    return high, (x - high.astype(F32)).astype(BF16)


def dot(left, right):
    return jnp.dot(left, right, preferred_element_type=F32)


def product(left, right):
    return dot(left[0], right[0]) + (dot(left[0], right[1]) + dot(left[1], right[0]))


def stacked_product(left, right):
    rows = left[0].shape[0]
    both = dot(jnp.concatenate(left, axis=0), right[0])
    return both[:rows] + (both[rows:] + dot(left[0], right[1]))


def identity(size):
    rows = lax.broadcasted_iota(jnp.int32, (size, size), 0)
    columns = lax.broadcasted_iota(jnp.int32, (size, size), 1)
    return (rows == columns).astype(F32)


def newton_batch(grams):
    eye = identity(grams[0].shape[0])
    count = range(len(grams))
    scales = [jnp.sqrt(jnp.sum(gram * gram)) + 1e-06 for gram in grams]
    once = [1.0 / scale for scale in scales]
    reciprocal = [1.0 / jnp.sqrt(scale) for scale in scales]
    power = [grams[i] * once[i] for i in count]
    start = [split(gram) for gram in grams]
    parts = start
    inverse = None
    for pair in range(NEWTON_STEPS // 2):
        square = [product(p, p) for p in parts]
        if pair == 0:
            square = [square[i] * (once[i] * once[i]) for i in count]
        square_parts = [split(p) for p in square]
        tail = [split(0.0625 * square[i] - 0.5625 * power[i]) for i in count]
        factor = [
            (2.25 * eye + (1.6875 * square[i] - 2.4375 * power[i]))
            + product(tail[i], square_parts[i])
            for i in count
        ]
        factor_parts = [split(q) for q in factor]
        if pair < NEWTON_STEPS // 2 - 1:
            twice = [split(product(q, q)) for q in factor_parts]
            power = [product(twice[i], parts[i]) for i in count]
            if pair == 0:
                power = [power[i] * once[i] for i in count]
            parts = [split(p) for p in power]
        if inverse is None:
            inverse = factor
            inverse_parts = factor_parts
        else:
            inverse = [product(inverse_parts[i], factor_parts[i]) for i in count]
            inverse_parts = [split(y) for y in inverse]
    basis = [inverse[i] * reciprocal[i] for i in count]
    root = [product(inverse_parts[i], start[i]) * reciprocal[i] for i in count]
    return basis, root


def newton_single(gram, beside=None):
    size = gram.shape[0]
    half = size // 2
    blocks = [slice(0, half), slice(half, size)]
    scale = jnp.sqrt(jnp.sum(gram * gram)) + 1e-06
    once, root_scale = 1.0 / scale, jnp.sqrt(scale)
    power, start = gram * once, split(gram)
    parts = start
    inverse = None
    for step in range(NEWTON_STEPS):
        left, right = (0.5 * once * once, 0.5 * once) if step == 0 else (0.5, 0.5)
        if step < NEWTON_STEPS - 1:
            first = [
                1.5 * power[rows]
                - left * stacked_product((parts[0][rows], parts[1][rows]), parts)
                for rows in blocks
            ]
        if beside is not None:
            beside(step)
        if step < NEWTON_STEPS - 1:
            following = jnp.concatenate(
                [1.5 * u - right * stacked_product(split(u), parts) for u in first], axis=0
            )
        if inverse is None:
            inverse = 1.5 * identity(size) - 0.5 * power
        else:
            inverse = jnp.concatenate(
                [
                    1.5 * inverse[rows]
                    - 0.5
                    * stacked_product((inverse_parts[0][rows], inverse_parts[1][rows]), parts)
                    for rows in blocks
                ],
                axis=0,
            )
        inverse_parts = split(inverse)
        if step < NEWTON_STEPS - 1:
            power = following
            parts = split(power)
    root = jnp.concatenate(
        [
            stacked_product((inverse_parts[0][rows], inverse_parts[1][rows]), start)
            for rows in blocks
        ],
        axis=0,
    )
    reciprocal = 1.0 / root_scale
    return inverse * reciprocal, root * reciprocal


def sibling_gram(low, high):
    low, high = split(low), split(high)
    half = low[0].shape[0] // 2
    wide = [jnp.concatenate([a, b], axis=1) for a, b in zip(low, high)]
    tall = [jnp.concatenate([a, b], axis=0) for a, b in zip(low, high)]
    return jnp.concatenate(
        [
            stacked_product((wide[0][rows], wide[1][rows]), tall)
            for rows in (slice(0, half), slice(half, None))
        ],
        axis=0,
    )


def packed(factor):
    half = factor.shape[0] // 2
    return jnp.concatenate([factor[:half, :half], factor[:half, half:], factor[half:, half:]], axis=0)


def unpacked(blocks):
    half = blocks.shape[1]
    first, cross, second = blocks[:half], blocks[half : 2 * half], blocks[2 * half :]
    upper = jnp.concatenate([first, cross], axis=1)
    return jnp.concatenate([upper, jnp.concatenate([cross.T, second], axis=1)], axis=0)


def edge_column(meta, leaves, index):
    column = meta[index]
    outside = jnp.logical_or(column < 0, column >= 2 * leaves)
    return outside, jnp.where(column < 0, column + NEAR, column - 2 * leaves)


def edge_leaf(meta, leaves, per_leaf, place):
    return jnp.where(meta[leaves * per_leaf] == 0, place, leaves - 1 - place)


def edge_plan(meta, leaves, per_leaf):
    plan = []
    beyond = jnp.int32(0)
    for place in range(leaves):
        leaf = edge_leaf(meta, leaves, per_leaf, place)
        most = leaves - place
        found = jnp.int32(0)
        slots = [jnp.int32(0)] * most
        columns = [jnp.int32(NEAR)] * most
        for slot in range(1, per_leaf):
            outside, column = edge_column(meta, leaves, leaf * per_leaf + slot)
            for item in range(most):
                hit = jnp.logical_and(outside, found == item)
                slots[item] = jnp.where(hit, slot, slots[item])
                columns[item] = jnp.where(hit, column, columns[item])
            found = found + outside.astype(jnp.int32)
        beyond = beyond + jnp.maximum(found - most, 0)
        plan.append((leaf, slots, columns))
    return plan, beyond


def inside_sum(
    meta, near, mine, sister, out, edge_blocks, window, held, sems, edge_sems, window_sems
):
    leaves, per_leaf = near.shape[0], near.shape[1]

    def inside(index):
        column = meta[index]
        return jnp.logical_and(column >= 0, column < 2 * leaves)

    def fetch(index):
        return pltpu.make_async_copy(
            near.at[index // per_leaf, index % per_leaf], held.at[index], sems.at[index]
        )

    core = meta[leaves * per_leaf]
    halves = [
        pltpu.make_async_copy(rows, window.at[pl.ds(place * leaves, leaves)], window_sems.at[number])
        for number, (rows, place) in enumerate(((mine, core), (sister, 1 - core)))
    ]
    for copy in halves:
        copy.start()
    for index in range(leaves * per_leaf):
        pl.when(inside(index))(fetch(index).start)
    plan, _ = edge_plan(meta, leaves, per_leaf)
    copies = []
    for leaf, slots, _ in plan:
        for slot in slots:
            index = len(copies)
            copies.append(
                pltpu.make_async_copy(
                    near.at[leaf, slot], edge_blocks.at[index], edge_sems.at[index]
                )
            )
            copies[-1].start()
    for copy in halves:
        copy.wait()

    def leaf_body(leaf, carry):
        base = leaf * per_leaf
        pltpu.make_async_copy(near.at[leaf, 0], held.at[base], sems.at[base]).wait()
        out[leaf] = dot(held[base], window[meta[base]])

        def block_body(slot, inner):
            index = base + slot

            @pl.when(inside(index))
            def _():
                pltpu.make_async_copy(
                    near.at[leaf, slot], held.at[index], sems.at[index]
                ).wait()
                out[leaf] += dot(held[index], window[meta[index]])

            return inner

        return lax.fori_loop(1, per_leaf, block_body, carry)

    lax.fori_loop(0, leaves, leaf_body, 0)
    for copy in copies:
        copy.wait()


def leaf_stage(
    meta, outer, partial, edge_blocks, near, bases, transfers, top, own, spare, sums, basis, merged, spare_sem, out_sems
):
    leaves, per_leaf = near.shape[0], near.shape[1]
    rank = partial.shape[2]
    half = partial.shape[1] // 2
    plan, beyond = edge_plan(meta, leaves, per_leaf)
    index = 0
    for leaf, _, columns in plan:
        blocks = [edge_blocks[index + item] for item in range(len(columns))]
        index += len(columns)
        windows = []
        for column in columns:
            window = outer[jnp.minimum(column, NEAR - 1)]
            windows.append(jnp.where(column < NEAR, window, jnp.zeros_like(window)))
        sums[leaf] = partial[leaf] + dot(
            jnp.concatenate(blocks, axis=1), jnp.concatenate(windows, axis=0)
        )

    @pl.when(beyond > 0)
    def _():
        def body(item, found):
            place, slot = item // (per_leaf - 1), 1 + item % (per_leaf - 1)
            leaf = edge_leaf(meta, leaves, per_leaf, place)
            found = jnp.where(slot == 1, 0, found)
            outside, column = edge_column(meta, leaves, leaf * per_leaf + slot)

            @pl.when(jnp.logical_and(outside, found >= leaves - place))
            def _():
                copy = pltpu.make_async_copy(near.at[leaf, slot], spare, spare_sem)
                copy.start()
                copy.wait()
                sums[leaf] += dot(spare[...], outer[column])

            return found + outside.astype(jnp.int32)

        lax.fori_loop(0, leaves * (per_leaf - 1), body, jnp.int32(0))

    grams = []
    for leaf in range(leaves):
        high, low = split(sums[leaf])
        turned = high.T
        cross = dot(turned, low)
        grams.append(dot(turned, high) + (cross + cross.T))
    inverse, factors = newton_batch(grams)

    later = []

    def leaf_basis(leaf, inverse_parts, part):
        rows = slice(part * half, (part + 1) * half)
        basis[leaf, rows] = product(split(sums[leaf, rows]), inverse_parts)
        if part == 1:
            pltpu.make_async_copy(basis.at[leaf], bases.at[leaf], out_sems.at[leaf]).start()

    def node_basis(slot, factor, inverse_parts, part):
        rows = slice(part * rank, (part + 1) * rank)
        merged[slot - 1, rows] = product(split(factor), inverse_parts)
        if part == 1:
            pltpu.make_async_copy(
                merged.at[slot - 1], transfers.at[slot], out_sems.at[leaves + slot - 1]
            ).start()

    for leaf in range(leaves):
        inverse_parts = split(inverse[leaf])
        for part in range(2):
            later.append((leaf_basis, leaf, inverse_parts, part))
    span = 1
    while len(factors) > 1:
        grams = [
            sibling_gram(factors[2 * node], factors[2 * node + 1])
            for node in range(len(factors) // 2)
        ]
        if len(grams) > 1:
            inverse, parents = newton_batch(grams)
        else:
            each = -(-len(later) // (NEWTON_STEPS - 1))

            def beside(step):
                for call, *arguments in later[step * each : (step + 1) * each]:
                    call(*arguments)

            single, parent = newton_single(grams[0], beside)
            inverse, parents = [single], [parent]
            top[...] = packed(parent)
            own[0], own[1], own[2] = factors[0], factors[1], single
        for node in range(len(grams) if len(grams) > 1 else 0):
            slot = node * 2 * span + span
            inverse_parts = split(inverse[node])
            for part in range(2):
                later.append((node_basis, slot, factors[2 * node + part], inverse_parts, part))
        factors = parents
        span *= 2
    for leaf in range(leaves):
        pltpu.make_async_copy(basis.at[leaf], bases.at[leaf], out_sems.at[leaf]).wait()
    for slot in range(1, leaves, 2):
        pltpu.make_async_copy(
            merged.at[slot - 1], transfers.at[slot], out_sems.at[leaves + slot - 1]
        ).wait()


def merge_stage(core, pair, factor, inverse):
    inverse[...], root = newton_single(sibling_gram(unpacked(pair[0]), unpacked(pair[1])))
    blocks = packed(root)
    half = blocks.shape[0] // 2
    factor[...] = jnp.where(core[0] == 0, blocks[:half], blocks[half:])


def first_merge_stage(core, pair, own, transfers_in, factor, inverse, transfers, merged, sem):
    del transfers_in
    rank = own.shape[1]
    slot = transfers.shape[0] // 2
    store = pltpu.make_async_copy(merged, transfers.at[slot], sem)

    def beside(step):
        if step in (2, 3):
            part = step - 2
            merged[part * rank : (part + 1) * rank] = product(split(own[part]), split(own[2]))
        if step == 3:
            store.start()

    inverse[...], root = newton_single(
        sibling_gram(unpacked(pair[0]), unpacked(pair[1])), beside
    )
    blocks = packed(root)
    half = blocks.shape[0] // 2
    factor[...] = jnp.where(core[0] == 0, blocks[:half], blocks[half:])
    store.wait()


def root_stage(scale, levels, meta, pair, *refs):
    pairs, inverses = refs[: levels - 1], refs[levels - 1 : 2 * levels - 2]
    transfers_in, transfers, root, own_pair, own_inverse, merged, sems = refs[2 * levels - 2 :]
    del transfers_in
    rank = root.shape[0]
    level = meta[0]
    fetched = jnp.where(jnp.logical_or(level == 0, level == levels), 1, level)

    def fetches(number):
        return (
            pltpu.make_async_copy(pairs[number - 1], own_pair, sems.at[0]),
            pltpu.make_async_copy(inverses[number - 1], own_inverse, sems.at[1]),
        )

    def node_basis(blocks, inverse_parts, part):
        rows = slice(part * rank, (part + 1) * rank)
        merged[rows] = product(split(unpacked(blocks)), inverse_parts)

    for number in range(1, levels):

        @pl.when(fetched == number)
        def _():
            for copy in fetches(number):
                copy.start()

    store = pltpu.make_async_copy(merged, transfers.at[0], sems.at[2])

    def beside(step):
        if step == 4:
            for copy in fetches(1):
                copy.wait()
        if step in (5, 6):
            own = own_inverse[...]
            own = jnp.where(level > 0, own, jnp.zeros_like(own))
            node_basis(own_pair[step - 5], split(own), step - 5)
        if step == 7:
            pl.when(level < levels)(store.start)

    inverse, factor = newton_single(sibling_gram(unpacked(pair[0]), unpacked(pair[1])), beside)
    root[...] = factor * scale

    @pl.when(level == levels)
    def _():
        for part in range(2):
            node_basis(pair[part], split(inverse), part)
        store.start()

    store.wait()


def spec(space):
    return pl.BlockSpec(memory_space=space)


def params(size):
    return pltpu.CompilerParams(vmem_limit_bytes=size * MIB)


def chip_groups(chips, bit):
    flip = (3 if bit % 2 else 1) << (bit - bit % 2)
    pairs = [(i, i ^ flip) for i in range(chips) if i & (1 << bit) == 0]
    return [[2 * i, 2 * i + 1, 2 * j, 2 * j + 1] for i, j in pairs]


def local(near_blocks, samples, pattern):
    leaves, per_leaf, leaf_size = near_blocks.shape[:3]
    rank = samples.shape[1]
    grp_count, dev_count = lax.axis_size("grp"), lax.axis_size("dev")
    devices = grp_count * dev_count
    device = lax.axis_index("grp") * dev_count + lax.axis_index("dev")
    chip, core = device // 2, device % 2
    edge = [(i, i + 1) for i in range(1, devices - 1, 2)]
    edge += [(j, i) for i, j in edge]
    outer = lax.ppermute(samples, ("grp", "dev"), edge)
    sister = lax.ppermute(samples, "dev", [(i, i ^ 1) for i in range(dev_count)])
    mine = samples.reshape(leaves, leaf_size, rank)
    sister = sister.reshape(leaves, leaf_size, rank)
    outer = outer.reshape(leaves, leaf_size, rank)

    own = core * leaves + jnp.arange(leaves, dtype=jnp.int32)[:, None]
    columns = jnp.concatenate([own, pattern - chip * 2 * leaves], axis=1).reshape(-1)
    meta = jnp.concatenate([columns, core[None].astype(jnp.int32)])

    leaf_sums = jax.ShapeDtypeStruct((leaves, leaf_size, rank), F32)
    blocks = leaves * per_leaf
    edges = leaves * (leaves + 1) // 2
    partial, edge_blocks = pl.pallas_call(
        inside_sum,
        out_shape=[leaf_sums, jax.ShapeDtypeStruct((edges, leaf_size, leaf_size), BF16)],
        in_specs=[spec(pltpu.SMEM)] + [spec(pl.ANY)] * 3,
        out_specs=[spec(pltpu.VMEM)] * 2,
        scratch_shapes=[
            pltpu.VMEM((2 * leaves, leaf_size, rank), BF16),
            pltpu.VMEM((blocks, leaf_size, leaf_size), BF16),
            pltpu.SemaphoreType.DMA((blocks,)),
            pltpu.SemaphoreType.DMA((edges,)),
            pltpu.SemaphoreType.DMA((2,)),
        ],
        compiler_params=params(44),
        cost_estimate=pl.CostEstimate(
            flops=2 * blocks * leaf_size * leaf_size * rank,
            bytes_accessed=2 * blocks * leaf_size * leaf_size,
            transcendentals=0,
        ),
        name="inside_sum",
    )(meta, near_blocks, mine, sister)

    square = jax.ShapeDtypeStruct((rank, rank), F32)
    half = rank // 2
    upper = jax.ShapeDtypeStruct((3 * half, half), F32)
    bases, transfers, factor, own_node = pl.pallas_call(
        leaf_stage,
        out_shape=[
            leaf_sums,
            jax.ShapeDtypeStruct((leaves, 2 * rank, rank), F32),
            upper,
            jax.ShapeDtypeStruct((3, rank, rank), F32),
        ],
        in_specs=[spec(pltpu.SMEM)] + [spec(pltpu.VMEM)] * 3 + [spec(pl.ANY)],
        out_specs=[spec(pl.ANY), spec(pl.ANY), spec(pltpu.VMEM), spec(pltpu.VMEM)],
        scratch_shapes=[
            pltpu.VMEM((leaf_size, leaf_size), BF16),
            pltpu.VMEM((leaves, leaf_size, rank), F32),
            pltpu.VMEM((leaves, leaf_size, rank), F32),
            pltpu.VMEM((leaves - 1, 2 * rank, rank), F32),
            pltpu.SemaphoreType.DMA,
            pltpu.SemaphoreType.DMA((2 * leaves - 1,)),
        ],
        compiler_params=params(44),
        name="leaf_stage",
    )(meta, outer, partial, edge_blocks, near_blocks)

    levels = devices.bit_length() - 1
    core_meta = core[None].astype(jnp.int32)
    pairs, inverses = [], []
    for number in range(levels):
        if number == 0:
            members = [[i, i + 1] for i in range(0, devices, 2)]
        else:
            members = chip_groups(devices // 2, number - 1)
        pair = lax.all_gather(factor, ("grp", "dev"), axis_index_groups=members)
        pair = pair.reshape(2, 3 * half, half)
        pairs.append(pair)
        part = jax.ShapeDtypeStruct((3 * half // 2, half), F32)
        if number == 0:
            factor, inverse, transfers = pl.pallas_call(
                first_merge_stage,
                out_shape=[part, square, jax.ShapeDtypeStruct(transfers.shape, F32)],
                in_specs=[spec(pltpu.SMEM)] + [spec(pltpu.VMEM)] * 2 + [spec(pl.ANY)],
                out_specs=[spec(pltpu.VMEM), spec(pltpu.VMEM), spec(pl.ANY)],
                scratch_shapes=[
                    pltpu.VMEM((2 * rank, rank), F32),
                    pltpu.SemaphoreType.DMA,
                ],
                input_output_aliases={3: 2},
                compiler_params=params(14),
                name="first_merge_stage",
            )(core_meta, pair, own_node, transfers)
            inverses.append(inverse)
        elif number < levels - 1:
            factor, inverse = pl.pallas_call(
                merge_stage,
                out_shape=[part, square],
                in_specs=[spec(pltpu.SMEM), spec(pltpu.VMEM)],
                out_specs=[spec(pltpu.VMEM), spec(pltpu.VMEM)],
                compiler_params=params(12),
                name="merge_stage",
            )(core_meta, pair)
            inverses.append(inverse)

    owned = jnp.int32(0)
    for number in range(1, levels + 1):
        is_owner = device & ((1 << number) - 1) == 1 << (number - 1)
        owned = jnp.where(is_owner, number, owned)
    total_rows = leaves * leaf_size * devices

    def root_body(*refs):
        root_stage(1.0 / math.sqrt(total_rows), levels, *refs)

    transfers, root = pl.pallas_call(
        root_body,
        out_shape=[jax.ShapeDtypeStruct((leaves, 2 * rank, rank), F32), square],
        in_specs=[spec(pltpu.SMEM), spec(pltpu.VMEM)] + [spec(pl.ANY)] * (2 * levels - 1),
        out_specs=[spec(pl.ANY), spec(pltpu.VMEM)],
        scratch_shapes=[
            pltpu.VMEM((2, 3 * half, half), F32),
            pltpu.VMEM((rank, rank), F32),
            pltpu.VMEM((2 * rank, rank), F32),
            pltpu.SemaphoreType.DMA((3,)),
        ],
        input_output_aliases={2 * levels: 0},
        compiler_params=params(14),
        name="root_stage",
    )(owned[None], pairs[-1], *pairs[:-1], *inverses, transfers)
    return (bases.reshape(leaves * leaf_size, rank), transfers, root)


def solution(mesh):
    in_specs = (
        P(("grp", "dev"), None, None, None),
        P(("grp", "dev"), None),
        P(("grp", "dev"), None),
    )
    out_specs = (P(("grp", "dev"), None), P(("grp", "dev"), None, None), P())
    return jax.shard_map(local, mesh=mesh, in_specs=in_specs, out_specs=out_specs, check_vma=False)
```

```python
import math

import jax
import jax.numpy as jnp
from jax import lax
from jax.experimental import pallas as pl
from jax.experimental.pallas import tpu as pltpu
from jax.sharding import PartitionSpec as P

NEAR = 4
NEWTON_STEPS = 10
BF16 = jnp.bfloat16
F32 = jnp.float32
MIB = 1 << 20


def split(x):
    high = x.astype(BF16)
    return high, (x - high.astype(F32)).astype(BF16)


def dot(left, right):
    return jnp.dot(left, right, preferred_element_type=F32)


def product(left, right):
    return dot(left[0], right[0]) + (dot(left[0], right[1]) + dot(left[1], right[0]))


def stacked_product(left, right):
    rows = left[0].shape[0]
    both = dot(jnp.concatenate(left, axis=0), right[0])
    return both[:rows] + (both[rows:] + dot(left[0], right[1]))


def identity(size):
    rows = lax.broadcasted_iota(jnp.int32, (size, size), 0)
    columns = lax.broadcasted_iota(jnp.int32, (size, size), 1)
    return (rows == columns).astype(F32)


def newton_batch(grams):
    eye = identity(grams[0].shape[0])
    count = range(len(grams))
    scales = [jnp.sqrt(jnp.sum(gram * gram)) + 1e-06 for gram in grams]
    once = [1.0 / scale for scale in scales]
    reciprocal = [1.0 / jnp.sqrt(scale) for scale in scales]
    power = [grams[i] * once[i] for i in count]
    start = [split(gram) for gram in grams]
    parts = start
    inverse = None
    for pair in range(NEWTON_STEPS // 2):
        square = [product(p, p) for p in parts]
        if pair == 0:
            square = [square[i] * (once[i] * once[i]) for i in count]
        square_parts = [split(p) for p in square]
        tail = [split(0.0625 * square[i] - 0.5625 * power[i]) for i in count]
        factor = [
            (2.25 * eye + (1.6875 * square[i] - 2.4375 * power[i]))
            + product(tail[i], square_parts[i])
            for i in count
        ]
        factor_parts = [split(q) for q in factor]
        if pair < NEWTON_STEPS // 2 - 1:
            twice = [split(product(q, q)) for q in factor_parts]
            power = [product(twice[i], parts[i]) for i in count]
            if pair == 0:
                power = [power[i] * once[i] for i in count]
            parts = [split(p) for p in power]
        if inverse is None:
            inverse = factor
            inverse_parts = factor_parts
        else:
            inverse = [product(inverse_parts[i], factor_parts[i]) for i in count]
            inverse_parts = [split(y) for y in inverse]
    basis = [inverse[i] * reciprocal[i] for i in count]
    root = [product(inverse_parts[i], start[i]) * reciprocal[i] for i in count]
    return basis, root


def newton_single(gram, beside=None):
    size = gram.shape[0]
    half = size // 2
    blocks = [slice(0, half), slice(half, size)]
    scale = jnp.sqrt(jnp.sum(gram * gram)) + 1e-06
    once, root_scale = 1.0 / scale, jnp.sqrt(scale)
    power, start = gram * once, split(gram)
    parts = start
    inverse = None
    for step in range(NEWTON_STEPS):
        left, right = (0.5 * once * once, 0.5 * once) if step == 0 else (0.5, 0.5)
        if step < NEWTON_STEPS - 1:
            first = [
                1.5 * power[rows]
                - left * stacked_product((parts[0][rows], parts[1][rows]), parts)
                for rows in blocks
            ]
        if beside is not None:
            beside(step)
        if step < NEWTON_STEPS - 1:
            following = jnp.concatenate(
                [1.5 * u - right * stacked_product(split(u), parts) for u in first], axis=0
            )
        if inverse is None:
            inverse = 1.5 * identity(size) - 0.5 * power
        else:
            inverse = jnp.concatenate(
                [
                    1.5 * inverse[rows]
                    - 0.5
                    * stacked_product((inverse_parts[0][rows], inverse_parts[1][rows]), parts)
                    for rows in blocks
                ],
                axis=0,
            )
        inverse_parts = split(inverse)
        if step < NEWTON_STEPS - 1:
            power = following
            parts = split(power)
    root = jnp.concatenate(
        [
            stacked_product((inverse_parts[0][rows], inverse_parts[1][rows]), start)
            for rows in blocks
        ],
        axis=0,
    )
    reciprocal = 1.0 / root_scale
    return inverse * reciprocal, root * reciprocal


def sibling_gram(low, high):
    low, high = split(low), split(high)
    half = low[0].shape[0] // 2
    wide = [jnp.concatenate([a, b], axis=1) for a, b in zip(low, high)]
    tall = [jnp.concatenate([a, b], axis=0) for a, b in zip(low, high)]
    return jnp.concatenate(
        [
            stacked_product((wide[0][rows], wide[1][rows]), tall)
            for rows in (slice(0, half), slice(half, None))
        ],
        axis=0,
    )


def packed(factor):
    half = factor.shape[0] // 2
    return jnp.concatenate([factor[:half, :half], factor[:half, half:], factor[half:, half:]], axis=0)


def unpacked(blocks):
    half = blocks.shape[1]
    first, cross, second = blocks[:half], blocks[half : 2 * half], blocks[2 * half :]
    upper = jnp.concatenate([first, cross], axis=1)
    return jnp.concatenate([upper, jnp.concatenate([cross.T, second], axis=1)], axis=0)


def edge_column(meta, leaves, index):
    column = meta[index]
    outside = jnp.logical_or(column < 0, column >= 2 * leaves)
    return outside, jnp.where(column < 0, column + NEAR, column - 2 * leaves)


def edge_leaf(meta, leaves, per_leaf, place):
    return jnp.where(meta[leaves * per_leaf] == 0, place, leaves - 1 - place)


def edge_plan(meta, leaves, per_leaf):
    plan = []
    beyond = jnp.int32(0)
    for place in range(leaves):
        leaf = edge_leaf(meta, leaves, per_leaf, place)
        most = leaves - place
        found = jnp.int32(0)
        slots = [jnp.int32(0)] * most
        columns = [jnp.int32(NEAR)] * most
        for slot in range(1, per_leaf):
            outside, column = edge_column(meta, leaves, leaf * per_leaf + slot)
            for item in range(most):
                hit = jnp.logical_and(outside, found == item)
                slots[item] = jnp.where(hit, slot, slots[item])
                columns[item] = jnp.where(hit, column, columns[item])
            found = found + outside.astype(jnp.int32)
        beyond = beyond + jnp.maximum(found - most, 0)
        plan.append((leaf, slots, columns))
    return plan, beyond


def inside_sum(
    meta, near, mine, sister, out, edge_blocks, window, held, sems, edge_sems, window_sems
):
    leaves, per_leaf = near.shape[0], near.shape[1]

    def inside(index):
        column = meta[index]
        return jnp.logical_and(column >= 0, column < 2 * leaves)

    def fetch(index):
        return pltpu.make_async_copy(
            near.at[index // per_leaf, index % per_leaf], held.at[index], sems.at[index]
        )

    core = meta[leaves * per_leaf]
    halves = [
        pltpu.make_async_copy(rows, window.at[pl.ds(place * leaves, leaves)], window_sems.at[number])
        for number, (rows, place) in enumerate(((mine, core), (sister, 1 - core)))
    ]
    for copy in halves:
        copy.start()
    for index in range(leaves * per_leaf):
        pl.when(inside(index))(fetch(index).start)
    plan, _ = edge_plan(meta, leaves, per_leaf)
    copies = []
    for leaf, slots, _ in plan:
        for slot in slots:
            index = len(copies)
            copies.append(
                pltpu.make_async_copy(
                    near.at[leaf, slot], edge_blocks.at[index], edge_sems.at[index]
                )
            )
            copies[-1].start()
    for copy in halves:
        copy.wait()

    def leaf_body(leaf, carry):
        base = leaf * per_leaf
        pltpu.make_async_copy(near.at[leaf, 0], held.at[base], sems.at[base]).wait()
        out[leaf] = dot(held[base], window[meta[base]])

        def block_body(slot, inner):
            index = base + slot

            @pl.when(inside(index))
            def _():
                pltpu.make_async_copy(
                    near.at[leaf, slot], held.at[index], sems.at[index]
                ).wait()
                out[leaf] += dot(held[index], window[meta[index]])

            return inner

        return lax.fori_loop(1, per_leaf, block_body, carry)

    lax.fori_loop(0, leaves, leaf_body, 0)
    for copy in copies:
        copy.wait()


def leaf_stage(
    meta, outer, partial, edge_blocks, near, bases, transfers, top, own, spare, sums, basis, merged, spare_sem, out_sems
):
    leaves, per_leaf = near.shape[0], near.shape[1]
    rank = partial.shape[2]
    half = partial.shape[1] // 2
    plan, beyond = edge_plan(meta, leaves, per_leaf)
    index = 0
    for leaf, _, columns in plan:
        blocks = [edge_blocks[index + item] for item in range(len(columns))]
        index += len(columns)
        windows = []
        for column in columns:
            window = outer[jnp.minimum(column, NEAR - 1)]
            windows.append(jnp.where(column < NEAR, window, jnp.zeros_like(window)))
        sums[leaf] = partial[leaf] + dot(
            jnp.concatenate(blocks, axis=1), jnp.concatenate(windows, axis=0)
        )

    @pl.when(beyond > 0)
    def _():
        def body(item, found):
            place, slot = item // (per_leaf - 1), 1 + item % (per_leaf - 1)
            leaf = edge_leaf(meta, leaves, per_leaf, place)
            found = jnp.where(slot == 1, 0, found)
            outside, column = edge_column(meta, leaves, leaf * per_leaf + slot)

            @pl.when(jnp.logical_and(outside, found >= leaves - place))
            def _():
                copy = pltpu.make_async_copy(near.at[leaf, slot], spare, spare_sem)
                copy.start()
                copy.wait()
                sums[leaf] += dot(spare[...], outer[column])

            return found + outside.astype(jnp.int32)

        lax.fori_loop(0, leaves * (per_leaf - 1), body, jnp.int32(0))

    grams = []
    for leaf in range(leaves):
        high, low = split(sums[leaf])
        turned = high.T
        cross = dot(turned, low)
        grams.append(dot(turned, high) + (cross + cross.T))
    inverse, factors = newton_batch(grams)

    later = []

    def leaf_basis(leaf, inverse_parts, part):
        rows = slice(part * half, (part + 1) * half)
        basis[leaf, rows] = product(split(sums[leaf, rows]), inverse_parts)
        if part == 1:
            pltpu.make_async_copy(basis.at[leaf], bases.at[leaf], out_sems.at[leaf]).start()

    def node_basis(slot, factor, inverse_parts, part):
        rows = slice(part * rank, (part + 1) * rank)
        merged[slot - 1, rows] = product(split(factor), inverse_parts)
        if part == 1:
            pltpu.make_async_copy(
                merged.at[slot - 1], transfers.at[slot], out_sems.at[leaves + slot - 1]
            ).start()

    for leaf in range(leaves):
        inverse_parts = split(inverse[leaf])
        for part in range(2):
            later.append((leaf_basis, leaf, inverse_parts, part))
    span = 1
    while len(factors) > 1:
        grams = [
            sibling_gram(factors[2 * node], factors[2 * node + 1])
            for node in range(len(factors) // 2)
        ]
        if len(grams) > 1:
            inverse, parents = newton_batch(grams)
        else:
            each = -(-len(later) // (NEWTON_STEPS - 1))

            def beside(step):
                for call, *arguments in later[step * each : (step + 1) * each]:
                    call(*arguments)

            single, parent = newton_single(grams[0], beside)
            inverse, parents = [single], [parent]
            top[...] = packed(parent)
            own[0], own[1], own[2] = factors[0], factors[1], single
        for node in range(len(grams) if len(grams) > 1 else 0):
            slot = node * 2 * span + span
            inverse_parts = split(inverse[node])
            for part in range(2):
                later.append((node_basis, slot, factors[2 * node + part], inverse_parts, part))
        factors = parents
        span *= 2
    for leaf in range(leaves):
        pltpu.make_async_copy(basis.at[leaf], bases.at[leaf], out_sems.at[leaf]).wait()
    for slot in range(1, leaves, 2):
        pltpu.make_async_copy(
            merged.at[slot - 1], transfers.at[slot], out_sems.at[leaves + slot - 1]
        ).wait()


def merge_stage(core, pair, factor, inverse):
    inverse[...], root = newton_single(sibling_gram(unpacked(pair[0]), unpacked(pair[1])))
    blocks = packed(root)
    half = blocks.shape[0] // 2
    factor[...] = jnp.where(core[0] == 0, blocks[:half], blocks[half:])


def first_merge_stage(core, pair, own, transfers_in, factor, inverse, transfers, merged, sem):
    del transfers_in
    rank = own.shape[1]
    slot = transfers.shape[0] // 2
    store = pltpu.make_async_copy(merged, transfers.at[slot], sem)

    def beside(step):
        if step in (2, 3):
            part = step - 2
            merged[part * rank : (part + 1) * rank] = product(split(own[part]), split(own[2]))
        if step == 3:
            store.start()

    inverse[...], root = newton_single(
        sibling_gram(unpacked(pair[0]), unpacked(pair[1])), beside
    )
    blocks = packed(root)
    half = blocks.shape[0] // 2
    factor[...] = jnp.where(core[0] == 0, blocks[:half], blocks[half:])
    store.wait()


def root_stage(scale, levels, meta, pair, *refs):
    pairs, inverses = refs[: levels - 1], refs[levels - 1 : 2 * levels - 2]
    transfers_in, transfers, root, own_pair, own_inverse, merged, sems = refs[2 * levels - 2 :]
    del transfers_in
    rank = root.shape[0]
    level = meta[0]
    fetched = jnp.where(jnp.logical_or(level == 0, level == levels), 1, level)

    def fetches(number):
        return (
            pltpu.make_async_copy(pairs[number - 1], own_pair, sems.at[0]),
            pltpu.make_async_copy(inverses[number - 1], own_inverse, sems.at[1]),
        )

    def node_basis(blocks, inverse_parts, part):
        rows = slice(part * rank, (part + 1) * rank)
        merged[rows] = product(split(unpacked(blocks)), inverse_parts)

    for number in range(1, levels):

        @pl.when(fetched == number)
        def _():
            for copy in fetches(number):
                copy.start()

    store = pltpu.make_async_copy(merged, transfers.at[0], sems.at[2])

    def beside(step):
        if step == 4:
            for copy in fetches(1):
                copy.wait()
        if step in (5, 6):
            own = own_inverse[...]
            own = jnp.where(level > 0, own, jnp.zeros_like(own))
            node_basis(own_pair[step - 5], split(own), step - 5)
        if step == 7:
            pl.when(level < levels)(store.start)

    inverse, factor = newton_single(sibling_gram(unpacked(pair[0]), unpacked(pair[1])), beside)
    root[...] = factor * scale

    @pl.when(level == levels)
    def _():
        for part in range(2):
            node_basis(pair[part], split(inverse), part)
        store.start()

    store.wait()


def spec(space):
    return pl.BlockSpec(memory_space=space)


def params(size):
    return pltpu.CompilerParams(vmem_limit_bytes=size * MIB)


def chip_groups(chips, bit):
    pairs = [(i, i ^ (1 << bit)) for i in range(chips) if i & (1 << bit) == 0]
    return [[2 * i, 2 * i + 1, 2 * j, 2 * j + 1] for i, j in pairs]


def local(near_blocks, samples, pattern):
    leaves, per_leaf, leaf_size = near_blocks.shape[:3]
    rank = samples.shape[1]
    grp_count, dev_count = lax.axis_size("grp"), lax.axis_size("dev")
    devices = grp_count * dev_count
    device = lax.axis_index("grp") * dev_count + lax.axis_index("dev")
    chip, core = device // 2, device % 2
    edge = [(i, i + 1) for i in range(1, devices - 1, 2)]
    edge += [(j, i) for i, j in edge]
    outer = lax.ppermute(samples, ("grp", "dev"), edge)
    sister = lax.ppermute(samples, "dev", [(i, i ^ 1) for i in range(dev_count)])
    mine = samples.reshape(leaves, leaf_size, rank)
    sister = sister.reshape(leaves, leaf_size, rank)
    outer = outer.reshape(leaves, leaf_size, rank)

    own = core * leaves + jnp.arange(leaves, dtype=jnp.int32)[:, None]
    columns = jnp.concatenate([own, pattern - chip * 2 * leaves], axis=1).reshape(-1)
    meta = jnp.concatenate([columns, core[None].astype(jnp.int32)])

    leaf_sums = jax.ShapeDtypeStruct((leaves, leaf_size, rank), F32)
    blocks = leaves * per_leaf
    edges = leaves * (leaves + 1) // 2
    partial, edge_blocks = pl.pallas_call(
        inside_sum,
        out_shape=[leaf_sums, jax.ShapeDtypeStruct((edges, leaf_size, leaf_size), BF16)],
        in_specs=[spec(pltpu.SMEM)] + [spec(pl.ANY)] * 3,
        out_specs=[spec(pltpu.VMEM)] * 2,
        scratch_shapes=[
            pltpu.VMEM((2 * leaves, leaf_size, rank), BF16),
            pltpu.VMEM((blocks, leaf_size, leaf_size), BF16),
            pltpu.SemaphoreType.DMA((blocks,)),
            pltpu.SemaphoreType.DMA((edges,)),
            pltpu.SemaphoreType.DMA((2,)),
        ],
        compiler_params=params(44),
        cost_estimate=pl.CostEstimate(
            flops=2 * blocks * leaf_size * leaf_size * rank,
            bytes_accessed=2 * blocks * leaf_size * leaf_size,
            transcendentals=0,
        ),
        name="inside_sum",
    )(meta, near_blocks, mine, sister)

    square = jax.ShapeDtypeStruct((rank, rank), F32)
    half = rank // 2
    upper = jax.ShapeDtypeStruct((3 * half, half), F32)
    bases, transfers, factor, own_node = pl.pallas_call(
        leaf_stage,
        out_shape=[
            leaf_sums,
            jax.ShapeDtypeStruct((leaves, 2 * rank, rank), F32),
            upper,
            jax.ShapeDtypeStruct((3, rank, rank), F32),
        ],
        in_specs=[spec(pltpu.SMEM)] + [spec(pltpu.VMEM)] * 3 + [spec(pl.ANY)],
        out_specs=[spec(pl.ANY), spec(pl.ANY), spec(pltpu.VMEM), spec(pltpu.VMEM)],
        scratch_shapes=[
            pltpu.VMEM((leaf_size, leaf_size), BF16),
            pltpu.VMEM((leaves, leaf_size, rank), F32),
            pltpu.VMEM((leaves, leaf_size, rank), F32),
            pltpu.VMEM((leaves - 1, 2 * rank, rank), F32),
            pltpu.SemaphoreType.DMA,
            pltpu.SemaphoreType.DMA((2 * leaves - 1,)),
        ],
        compiler_params=params(44),
        name="leaf_stage",
    )(meta, outer, partial, edge_blocks, near_blocks)

    levels = devices.bit_length() - 1
    core_meta = core[None].astype(jnp.int32)
    pairs, inverses = [], []
    for number in range(levels):
        if number == 0:
            members = [[i, i + 1] for i in range(0, devices, 2)]
        else:
            members = chip_groups(devices // 2, number - 1)
        pair = lax.all_gather(factor, ("grp", "dev"), axis_index_groups=members)
        pair = pair.reshape(2, 3 * half, half)
        pairs.append(pair)
        part = jax.ShapeDtypeStruct((3 * half // 2, half), F32)
        if number == 0:
            factor, inverse, transfers = pl.pallas_call(
                first_merge_stage,
                out_shape=[part, square, jax.ShapeDtypeStruct(transfers.shape, F32)],
                in_specs=[spec(pltpu.SMEM)] + [spec(pltpu.VMEM)] * 2 + [spec(pl.ANY)],
                out_specs=[spec(pltpu.VMEM), spec(pltpu.VMEM), spec(pl.ANY)],
                scratch_shapes=[
                    pltpu.VMEM((2 * rank, rank), F32),
                    pltpu.SemaphoreType.DMA,
                ],
                input_output_aliases={3: 2},
                compiler_params=params(14),
                name="first_merge_stage",
            )(core_meta, pair, own_node, transfers)
            inverses.append(inverse)
        elif number < levels - 1:
            factor, inverse = pl.pallas_call(
                merge_stage,
                out_shape=[part, square],
                in_specs=[spec(pltpu.SMEM), spec(pltpu.VMEM)],
                out_specs=[spec(pltpu.VMEM), spec(pltpu.VMEM)],
                compiler_params=params(12),
                name="merge_stage",
            )(core_meta, pair)
            inverses.append(inverse)

    owned = jnp.int32(0)
    for number in range(1, levels + 1):
        is_owner = device & ((1 << number) - 1) == 1 << (number - 1)
        owned = jnp.where(is_owner, number, owned)
    total_rows = leaves * leaf_size * devices

    def root_body(*refs):
        root_stage(1.0 / math.sqrt(total_rows), levels, *refs)

    transfers, root = pl.pallas_call(
        root_body,
        out_shape=[jax.ShapeDtypeStruct((leaves, 2 * rank, rank), F32), square],
        in_specs=[spec(pltpu.SMEM), spec(pltpu.VMEM)] + [spec(pl.ANY)] * (2 * levels - 1),
        out_specs=[spec(pl.ANY), spec(pltpu.VMEM)],
        scratch_shapes=[
            pltpu.VMEM((2, 3 * half, half), F32),
            pltpu.VMEM((rank, rank), F32),
            pltpu.VMEM((2 * rank, rank), F32),
            pltpu.SemaphoreType.DMA((3,)),
        ],
        input_output_aliases={2 * levels: 0},
        compiler_params=params(14),
        name="root_stage",
    )(owned[None], pairs[-1], *pairs[:-1], *inverses, transfers)
    return (bases.reshape(leaves * leaf_size, rank), transfers, root)


def solution(mesh):
    in_specs = (
        P(("grp", "dev"), None, None, None),
        P(("grp", "dev"), None),
        P(("grp", "dev"), None),
    )
    out_specs = (P(("grp", "dev"), None), P(("grp", "dev"), None, None), P())
    return jax.shard_map(local, mesh=mesh, in_specs=in_specs, out_specs=out_specs, check_vma=False)
```

```python
import math

import jax
import jax.numpy as jnp
from jax import lax
from jax.experimental import pallas as pl
from jax.experimental.pallas import tpu as pltpu
from jax.sharding import PartitionSpec as P

NEAR = 4
NEWTON_STEPS = 10
BF16 = jnp.bfloat16
F32 = jnp.float32
MIB = 1 << 20


def split(x):
    high = x.astype(BF16)
    return high, (x - high.astype(F32)).astype(BF16)


def dot(left, right):
    return jnp.dot(left, right, preferred_element_type=F32)


def product(left, right):
    return dot(left[0], right[0]) + (dot(left[0], right[1]) + dot(left[1], right[0]))


def stacked_product(left, right):
    rows = left[0].shape[0]
    both = dot(jnp.concatenate(left, axis=0), right[0])
    return both[:rows] + (both[rows:] + dot(left[0], right[1]))


def identity(size):
    rows = lax.broadcasted_iota(jnp.int32, (size, size), 0)
    columns = lax.broadcasted_iota(jnp.int32, (size, size), 1)
    return (rows == columns).astype(F32)


def newton_batch(grams):
    eye = identity(grams[0].shape[0])
    count = range(len(grams))
    scales = [jnp.sqrt(jnp.sum(gram * gram)) + 1e-06 for gram in grams]
    once = [1.0 / scale for scale in scales]
    reciprocal = [1.0 / jnp.sqrt(scale) for scale in scales]
    power = [grams[i] * once[i] for i in count]
    start = [split(gram) for gram in grams]
    parts = start
    inverse = None
    for pair in range(NEWTON_STEPS // 2):
        square = [product(p, p) for p in parts]
        if pair == 0:
            square = [square[i] * (once[i] * once[i]) for i in count]
        square_parts = [split(p) for p in square]
        tail = [split(0.0625 * square[i] - 0.5625 * power[i]) for i in count]
        factor = [
            (2.25 * eye + (1.6875 * square[i] - 2.4375 * power[i]))
            + product(tail[i], square_parts[i])
            for i in count
        ]
        factor_parts = [split(q) for q in factor]
        if pair < NEWTON_STEPS // 2 - 1:
            twice = [split(product(q, q)) for q in factor_parts]
            power = [product(twice[i], parts[i]) for i in count]
            if pair == 0:
                power = [power[i] * once[i] for i in count]
            parts = [split(p) for p in power]
        if inverse is None:
            inverse = factor
            inverse_parts = factor_parts
        else:
            inverse = [product(inverse_parts[i], factor_parts[i]) for i in count]
            inverse_parts = [split(y) for y in inverse]
    basis = [inverse[i] * reciprocal[i] for i in count]
    root = [product(inverse_parts[i], start[i]) * reciprocal[i] for i in count]
    return basis, root


def newton_single(gram, beside=None):
    size = gram.shape[0]
    half = size // 2
    blocks = [slice(0, half), slice(half, size)]
    scale = jnp.sqrt(jnp.sum(gram * gram)) + 1e-06
    once, root_scale = 1.0 / scale, jnp.sqrt(scale)
    power, start = gram * once, split(gram)
    parts = start
    inverse = None
    for step in range(NEWTON_STEPS):
        left, right = (0.5 * once * once, 0.5 * once) if step == 0 else (0.5, 0.5)
        if step < NEWTON_STEPS - 1:
            first = [
                1.5 * power[rows]
                - left * stacked_product((parts[0][rows], parts[1][rows]), parts)
                for rows in blocks
            ]
        if beside is not None:
            beside(step)
        if step < NEWTON_STEPS - 1:
            following = jnp.concatenate(
                [1.5 * u - right * stacked_product(split(u), parts) for u in first], axis=0
            )
        if inverse is None:
            inverse = 1.5 * identity(size) - 0.5 * power
        else:
            inverse = jnp.concatenate(
                [
                    1.5 * inverse[rows]
                    - 0.5
                    * stacked_product((inverse_parts[0][rows], inverse_parts[1][rows]), parts)
                    for rows in blocks
                ],
                axis=0,
            )
        inverse_parts = split(inverse)
        if step < NEWTON_STEPS - 1:
            power = following
            parts = split(power)
    root = jnp.concatenate(
        [
            stacked_product((inverse_parts[0][rows], inverse_parts[1][rows]), start)
            for rows in blocks
        ],
        axis=0,
    )
    reciprocal = 1.0 / root_scale
    return inverse * reciprocal, root * reciprocal


def sibling_gram(low, high):
    low, high = split(low), split(high)
    half = low[0].shape[0] // 2
    wide = [jnp.concatenate([a, b], axis=1) for a, b in zip(low, high)]
    tall = [jnp.concatenate([a, b], axis=0) for a, b in zip(low, high)]
    return jnp.concatenate(
        [
            stacked_product((wide[0][rows], wide[1][rows]), tall)
            for rows in (slice(0, half), slice(half, None))
        ],
        axis=0,
    )


def packed(factor):
    half = factor.shape[0] // 2
    return jnp.concatenate([factor[:half, :half], factor[:half, half:], factor[half:, half:]], axis=0)


def unpacked(blocks):
    half = blocks.shape[1]
    first, cross, second = blocks[:half], blocks[half : 2 * half], blocks[2 * half :]
    upper = jnp.concatenate([first, cross], axis=1)
    return jnp.concatenate([upper, jnp.concatenate([cross.T, second], axis=1)], axis=0)


def edge_column(meta, leaves, index):
    column = meta[index]
    outside = jnp.logical_or(column < 0, column >= 2 * leaves)
    return outside, jnp.where(column < 0, column + NEAR, column - 2 * leaves)


def edge_leaf(meta, leaves, per_leaf, place):
    return jnp.where(meta[leaves * per_leaf] == 0, place, leaves - 1 - place)


def edge_plan(meta, leaves, per_leaf):
    plan = []
    beyond = jnp.int32(0)
    for place in range(leaves):
        leaf = edge_leaf(meta, leaves, per_leaf, place)
        most = leaves - place
        found = jnp.int32(0)
        slots = [jnp.int32(0)] * most
        columns = [jnp.int32(NEAR)] * most
        for slot in range(1, per_leaf):
            outside, column = edge_column(meta, leaves, leaf * per_leaf + slot)
            for item in range(most):
                hit = jnp.logical_and(outside, found == item)
                slots[item] = jnp.where(hit, slot, slots[item])
                columns[item] = jnp.where(hit, column, columns[item])
            found = found + outside.astype(jnp.int32)
        beyond = beyond + jnp.maximum(found - most, 0)
        plan.append((leaf, slots, columns))
    return plan, beyond


def inside_sum(
    meta, near, mine, sister, out, edge_blocks, window, held, sems, edge_sems, window_sems
):
    leaves, per_leaf = near.shape[0], near.shape[1]

    def inside(index):
        column = meta[index]
        return jnp.logical_and(column >= 0, column < 2 * leaves)

    def fetch(index):
        return pltpu.make_async_copy(
            near.at[index // per_leaf, index % per_leaf], held.at[index], sems.at[index]
        )

    core = meta[leaves * per_leaf]
    halves = [
        pltpu.make_async_copy(rows, window.at[pl.ds(place * leaves, leaves)], window_sems.at[number])
        for number, (rows, place) in enumerate(((mine, core), (sister, 1 - core)))
    ]
    for copy in halves:
        copy.start()
    for index in range(leaves * per_leaf):
        pl.when(inside(index))(fetch(index).start)
    plan, _ = edge_plan(meta, leaves, per_leaf)
    copies = []
    for leaf, slots, _ in plan:
        for slot in slots:
            index = len(copies)
            copies.append(
                pltpu.make_async_copy(
                    near.at[leaf, slot], edge_blocks.at[index], edge_sems.at[index]
                )
            )
            copies[-1].start()
    for copy in halves:
        copy.wait()

    def leaf_body(leaf, carry):
        base = leaf * per_leaf
        pltpu.make_async_copy(near.at[leaf, 0], held.at[base], sems.at[base]).wait()
        out[leaf] = dot(held[base], window[meta[base]])

        def block_body(slot, inner):
            index = base + slot

            @pl.when(inside(index))
            def _():
                pltpu.make_async_copy(
                    near.at[leaf, slot], held.at[index], sems.at[index]
                ).wait()
                out[leaf] += dot(held[index], window[meta[index]])

            return inner

        return lax.fori_loop(1, per_leaf, block_body, carry)

    lax.fori_loop(0, leaves, leaf_body, 0)
    for copy in copies:
        copy.wait()


def leaf_stage(
    meta, outer, partial, edge_blocks, near, bases, transfers, top, own, spare, sums, basis, merged, spare_sem, out_sems
):
    leaves, per_leaf = near.shape[0], near.shape[1]
    rank = partial.shape[2]
    half = partial.shape[1] // 2
    plan, beyond = edge_plan(meta, leaves, per_leaf)
    index = 0
    for leaf, _, columns in plan:
        blocks = [edge_blocks[index + item] for item in range(len(columns))]
        index += len(columns)
        windows = []
        for column in columns:
            window = outer[jnp.minimum(column, NEAR - 1)]
            windows.append(jnp.where(column < NEAR, window, jnp.zeros_like(window)))
        sums[leaf] = partial[leaf] + dot(
            jnp.concatenate(blocks, axis=1), jnp.concatenate(windows, axis=0)
        )

    @pl.when(beyond > 0)
    def _():
        def body(item, found):
            place, slot = item // (per_leaf - 1), 1 + item % (per_leaf - 1)
            leaf = edge_leaf(meta, leaves, per_leaf, place)
            found = jnp.where(slot == 1, 0, found)
            outside, column = edge_column(meta, leaves, leaf * per_leaf + slot)

            @pl.when(jnp.logical_and(outside, found >= leaves - place))
            def _():
                copy = pltpu.make_async_copy(near.at[leaf, slot], spare, spare_sem)
                copy.start()
                copy.wait()
                sums[leaf] += dot(spare[...], outer[column])

            return found + outside.astype(jnp.int32)

        lax.fori_loop(0, leaves * (per_leaf - 1), body, jnp.int32(0))

    grams = []
    for leaf in range(leaves):
        high, low = split(sums[leaf])
        turned = high.T
        cross = dot(turned, low)
        grams.append(dot(turned, high) + (cross + cross.T))
    inverse, factors = newton_batch(grams)

    later = []

    def leaf_basis(leaf, inverse_parts, part):
        rows = slice(part * half, (part + 1) * half)
        basis[leaf, rows] = product(split(sums[leaf, rows]), inverse_parts)
        if part == 1:
            pltpu.make_async_copy(basis.at[leaf], bases.at[leaf], out_sems.at[leaf]).start()

    def node_basis(slot, factor, inverse_parts, part):
        rows = slice(part * rank, (part + 1) * rank)
        merged[slot - 1, rows] = product(split(factor), inverse_parts)
        if part == 1:
            pltpu.make_async_copy(
                merged.at[slot - 1], transfers.at[slot], out_sems.at[leaves + slot - 1]
            ).start()

    for leaf in range(leaves):
        inverse_parts = split(inverse[leaf])
        for part in range(2):
            later.append((leaf_basis, leaf, inverse_parts, part))
    span = 1
    while len(factors) > 1:
        grams = [
            sibling_gram(factors[2 * node], factors[2 * node + 1])
            for node in range(len(factors) // 2)
        ]
        if len(grams) > 1:
            inverse, parents = newton_batch(grams)
        else:
            each = -(-len(later) // (NEWTON_STEPS - 1))

            def beside(step):
                for call, *arguments in later[step * each : (step + 1) * each]:
                    call(*arguments)

            single, parent = newton_single(grams[0], beside)
            inverse, parents = [single], [parent]
            top[...] = packed(parent)
            own[0], own[1], own[2] = factors[0], factors[1], single
        for node in range(len(grams) if len(grams) > 1 else 0):
            slot = node * 2 * span + span
            inverse_parts = split(inverse[node])
            for part in range(2):
                later.append((node_basis, slot, factors[2 * node + part], inverse_parts, part))
        factors = parents
        span *= 2
    for leaf in range(leaves):
        pltpu.make_async_copy(basis.at[leaf], bases.at[leaf], out_sems.at[leaf]).wait()
    for slot in range(1, leaves, 2):
        pltpu.make_async_copy(
            merged.at[slot - 1], transfers.at[slot], out_sems.at[leaves + slot - 1]
        ).wait()


def merge_stage(core, pair, factor, inverse):
    inverse[...], root = newton_single(sibling_gram(unpacked(pair[0]), unpacked(pair[1])))
    blocks = packed(root)
    half = blocks.shape[0] // 2
    factor[...] = jnp.where(core[0] == 0, blocks[:half], blocks[half:])


def first_merge_stage(core, pair, own, transfers_in, factor, inverse, transfers, merged, sem):
    del transfers_in
    rank = own.shape[1]
    slot = transfers.shape[0] // 2
    store = pltpu.make_async_copy(merged, transfers.at[slot], sem)

    def beside(step):
        if step in (2, 3):
            part = step - 2
            merged[part * rank : (part + 1) * rank] = product(split(own[part]), split(own[2]))
        if step == 3:
            store.start()

    inverse[...], root = newton_single(
        sibling_gram(unpacked(pair[0]), unpacked(pair[1])), beside
    )
    blocks = packed(root)
    half = blocks.shape[0] // 2
    factor[...] = jnp.where(core[0] == 0, blocks[:half], blocks[half:])
    store.wait()


def root_stage(scale, levels, meta, pair, *refs):
    pairs, inverses = refs[: levels - 1], refs[levels - 1 : 2 * levels - 2]
    transfers_in, transfers, root, own_pair, own_inverse, merged, last, sems = refs[2 * levels - 2 :]
    del transfers_in
    rank = root.shape[0]
    level = meta[0]
    fetched = jnp.where(jnp.logical_or(level == 0, level == levels), 1, level)

    def fetches(number):
        return (
            pltpu.make_async_copy(pairs[number - 1], own_pair, sems.at[0]),
            pltpu.make_async_copy(inverses[number - 1], own_inverse, sems.at[1]),
        )

    def node_basis(target, blocks, inverse_parts, part):
        rows = slice(part * rank, (part + 1) * rank)
        target[rows] = product(split(unpacked(blocks)), inverse_parts)

    for number in range(1, levels):

        @pl.when(fetched == number)
        def _():
            for copy in fetches(number):
                copy.start()

    store = pltpu.make_async_copy(merged, transfers.at[0], sems.at[2])

    def beside(step):
        if step == 4:
            for copy in fetches(1):
                copy.wait()
        if step in (5, 6):
            own = own_inverse[...]
            own = jnp.where(level > 0, own, jnp.zeros_like(own))
            node_basis(merged, own_pair[step - 5], split(own), step - 5)
        if step == 7:
            pl.when(level < levels)(store.start)

    inverse, factor = newton_single(sibling_gram(unpacked(pair[0]), unpacked(pair[1])), beside)
    root[...] = factor * scale
    inverse_parts = split(inverse)
    for part in range(2):
        node_basis(last, pair[part], inverse_parts, part)
    store_last = pltpu.make_async_copy(last, transfers.at[0], sems.at[2])
    pl.when(level == levels)(store_last.start)
    store.wait()


def spec(space):
    return pl.BlockSpec(memory_space=space)


def params(size):
    return pltpu.CompilerParams(vmem_limit_bytes=size * MIB)


def chip_groups(chips, bit):
    flip = (3 if bit % 2 else 1) << (bit - bit % 2)
    pairs = [(i, i ^ flip) for i in range(chips) if i & (1 << bit) == 0]
    return [[2 * i, 2 * i + 1, 2 * j, 2 * j + 1] for i, j in pairs]


def local(near_blocks, samples, pattern):
    leaves, per_leaf, leaf_size = near_blocks.shape[:3]
    rank = samples.shape[1]
    grp_count, dev_count = lax.axis_size("grp"), lax.axis_size("dev")
    devices = grp_count * dev_count
    device = lax.axis_index("grp") * dev_count + lax.axis_index("dev")
    chip, core = device // 2, device % 2
    edge = [(i, i + 1) for i in range(1, devices - 1, 2)]
    edge += [(j, i) for i, j in edge]
    outer = lax.ppermute(samples, ("grp", "dev"), edge)
    sister = lax.ppermute(samples, "dev", [(i, i ^ 1) for i in range(dev_count)])
    mine = samples.reshape(leaves, leaf_size, rank)
    sister = sister.reshape(leaves, leaf_size, rank)
    outer = outer.reshape(leaves, leaf_size, rank)

    own = core * leaves + jnp.arange(leaves, dtype=jnp.int32)[:, None]
    columns = jnp.concatenate([own, pattern - chip * 2 * leaves], axis=1).reshape(-1)
    meta = jnp.concatenate([columns, core[None].astype(jnp.int32)])

    leaf_sums = jax.ShapeDtypeStruct((leaves, leaf_size, rank), F32)
    blocks = leaves * per_leaf
    edges = leaves * (leaves + 1) // 2
    partial, edge_blocks = pl.pallas_call(
        inside_sum,
        out_shape=[leaf_sums, jax.ShapeDtypeStruct((edges, leaf_size, leaf_size), BF16)],
        in_specs=[spec(pltpu.SMEM)] + [spec(pl.ANY)] * 3,
        out_specs=[spec(pltpu.VMEM)] * 2,
        scratch_shapes=[
            pltpu.VMEM((2 * leaves, leaf_size, rank), BF16),
            pltpu.VMEM((blocks, leaf_size, leaf_size), BF16),
            pltpu.SemaphoreType.DMA((blocks,)),
            pltpu.SemaphoreType.DMA((edges,)),
            pltpu.SemaphoreType.DMA((2,)),
        ],
        compiler_params=params(44),
        cost_estimate=pl.CostEstimate(
            flops=2 * blocks * leaf_size * leaf_size * rank,
            bytes_accessed=2 * blocks * leaf_size * leaf_size,
            transcendentals=0,
        ),
        name="inside_sum",
    )(meta, near_blocks, mine, sister)

    square = jax.ShapeDtypeStruct((rank, rank), F32)
    half = rank // 2
    upper = jax.ShapeDtypeStruct((3 * half, half), F32)
    bases, transfers, factor, own_node = pl.pallas_call(
        leaf_stage,
        out_shape=[
            leaf_sums,
            jax.ShapeDtypeStruct((leaves, 2 * rank, rank), F32),
            upper,
            jax.ShapeDtypeStruct((3, rank, rank), F32),
        ],
        in_specs=[spec(pltpu.SMEM)] + [spec(pltpu.VMEM)] * 3 + [spec(pl.ANY)],
        out_specs=[spec(pl.ANY), spec(pl.ANY), spec(pltpu.VMEM), spec(pltpu.VMEM)],
        scratch_shapes=[
            pltpu.VMEM((leaf_size, leaf_size), BF16),
            pltpu.VMEM((leaves, leaf_size, rank), F32),
            pltpu.VMEM((leaves, leaf_size, rank), F32),
            pltpu.VMEM((leaves - 1, 2 * rank, rank), F32),
            pltpu.SemaphoreType.DMA,
            pltpu.SemaphoreType.DMA((2 * leaves - 1,)),
        ],
        compiler_params=params(44),
        name="leaf_stage",
    )(meta, outer, partial, edge_blocks, near_blocks)

    levels = devices.bit_length() - 1
    core_meta = core[None].astype(jnp.int32)
    pairs, inverses = [], []
    for number in range(levels):
        if number == 0:
            members = [[i, i + 1] for i in range(0, devices, 2)]
        else:
            members = chip_groups(devices // 2, number - 1)
        pair = lax.all_gather(factor, ("grp", "dev"), axis_index_groups=members)
        pair = pair.reshape(2, 3 * half, half)
        pairs.append(pair)
        part = jax.ShapeDtypeStruct((3 * half // 2, half), F32)
        if number == 0:
            factor, inverse, transfers = pl.pallas_call(
                first_merge_stage,
                out_shape=[part, square, jax.ShapeDtypeStruct(transfers.shape, F32)],
                in_specs=[spec(pltpu.SMEM)] + [spec(pltpu.VMEM)] * 2 + [spec(pl.ANY)],
                out_specs=[spec(pltpu.VMEM), spec(pltpu.VMEM), spec(pl.ANY)],
                scratch_shapes=[
                    pltpu.VMEM((2 * rank, rank), F32),
                    pltpu.SemaphoreType.DMA,
                ],
                input_output_aliases={3: 2},
                compiler_params=params(14),
                name="first_merge_stage",
            )(core_meta, pair, own_node, transfers)
            inverses.append(inverse)
        elif number < levels - 1:
            factor, inverse = pl.pallas_call(
                merge_stage,
                out_shape=[part, square],
                in_specs=[spec(pltpu.SMEM), spec(pltpu.VMEM)],
                out_specs=[spec(pltpu.VMEM), spec(pltpu.VMEM)],
                compiler_params=params(12),
                name="merge_stage",
            )(core_meta, pair)
            inverses.append(inverse)

    owned = jnp.int32(0)
    for number in range(1, levels + 1):
        is_owner = device & ((1 << number) - 1) == 1 << (number - 1)
        owned = jnp.where(is_owner, number, owned)
    total_rows = leaves * leaf_size * devices

    def root_body(*refs):
        root_stage(1.0 / math.sqrt(total_rows), levels, *refs)

    transfers, root = pl.pallas_call(
        root_body,
        out_shape=[jax.ShapeDtypeStruct((leaves, 2 * rank, rank), F32), square],
        in_specs=[spec(pltpu.SMEM), spec(pltpu.VMEM)] + [spec(pl.ANY)] * (2 * levels - 1),
        out_specs=[spec(pl.ANY), spec(pltpu.VMEM)],
        scratch_shapes=[
            pltpu.VMEM((2, 3 * half, half), F32),
            pltpu.VMEM((rank, rank), F32),
            pltpu.VMEM((2 * rank, rank), F32),
            pltpu.VMEM((2 * rank, rank), F32),
            pltpu.SemaphoreType.DMA((3,)),
        ],
        input_output_aliases={2 * levels: 0},
        compiler_params=params(14),
        name="root_stage",
    )(owned[None], pairs[-1], *pairs[:-1], *inverses, transfers)
    return (bases.reshape(leaves * leaf_size, rank), transfers, root)


def solution(mesh):
    in_specs = (
        P(("grp", "dev"), None, None, None),
        P(("grp", "dev"), None),
        P(("grp", "dev"), None),
    )
    out_specs = (P(("grp", "dev"), None), P(("grp", "dev"), None, None), P())
    return jax.shard_map(local, mesh=mesh, in_specs=in_specs, out_specs=out_specs, check_vma=False)
```
